32 devices in a mesh: dp: 4 (over x, core), tp: 8 (over z, y).
Axes of the slice: x: 2, y: 2, z: 4, core: 2. Of those that a mesh axis runs over, the one named last changes fastest.
Arguments:
- out_grad: bfloat16 [512, 7168], P(('dp', 'tp')), may hold values from -1.5 to 1.5
- gate_pre: bfloat16 [512, 12288], P('dp', 'tp'), may hold values from -8 to 8
- up_pre: bfloat16 [512, 12288], P('dp', 'tp'), may hold values from -6 to 6
- down_weight: bfloat16 [7168, 12288], P(None, 'tp'), may hold values from -0.0625 to 0.0625
- block_scales: bfloat16 [56, 96], P(None, 'tp'), may hold values from 0.25 to 4
Outputs:
- gate_grad: bfloat16 [512, 12288], P('dp', 'tp')
- up_grad: bfloat16 [512, 12288], P('dp', 'tp')
- down_grad: bfloat16 [7168, 12288], P('dp', 'tp')
The draws below stay inside these ranges and needn't reach their ends.
All inputs are finite; a program needn't handle non-finite values.
Results may differ from the reference program's by a relative error of at most 0.028.
Values may be sent and summed in bfloat16 or wider, within the bound.
No kernel may reach another device: no remote copies, remote signals or barrier semaphores. Data moves between devices by JAX's collectives and lax.ppermute only.
A program may use at most 128 MiB of HBM per device.

```python
import math
import jax
import jax.numpy as jnp
from jax import lax

D = 7168
FF = 12288
TOK = 128
TOKENS = 512
N_DP = 4


def strengthened(values, key, source, target, blocks, factor):
    owner, partner = [(jnp.arange(values.shape[position]) // (values.shape[position] // blocks)).reshape([-1 if axis == position else 1 for axis in range(values.ndim)]) for position in (source, target)]
    chosen = jax.random.permutation(key, blocks)[partner]
    strong = (owner == chosen) | (owner == (partner + blocks // 2) % blocks)
    return jnp.where(strong, factor * values, values)


def level_of(stream_key, dims, cuts, smallest, high):
    def one(dim, blocks):
        steps = jax.random.uniform(jax.random.fold_in(jax.random.fold_in(stream_key, 6), dim), (blocks,), jnp.float32, smallest / len(cuts), high / len(cuts))
        return jnp.repeat(jnp.exp(steps), dims[dim] // blocks).reshape((-1,) + (1,) * (len(dims) - dim - 1))

    gain = one(*cuts[0])
    for cut in cuts[1:]:
        gain = gain * one(*cut)
    return gain


def normal_values(rng, dims, deviation, most, split=(), held_as=jnp.bfloat16):
    factor_of = level_of(rng, dims, split, -0.22, 0.18) if split else 1.0
    array = jax.random.normal(rng, dims, jnp.float32) * deviation * factor_of
    return jnp.minimum(jnp.maximum(array, -most), most).astype(held_as)


def gaussian_with(key, dims, scale, most, pieces, heavy, kind=jnp.bfloat16):
    entries = scale * jax.random.normal(key, dims, jnp.float32)
    if pieces:
        entries = entries * level_of(key, dims, pieces, -0.22, 0.18)
    return jnp.clip(strengthened(entries, jax.random.fold_in(key, 3), *heavy), -most, most).astype(kind)


def setup_inputs(seed: int = 0) -> dict:
    seeds = jax.random.split(jax.random.key(seed), 6)
    return {
        "out_grad": gaussian_with(seeds[0], (TOKENS, D), 0.25, 1.5, ((0, 32),), (0, 1, 32, 2.75)),
        "gate_pre": normal_values(seeds[1], (TOKENS, FF), 1.5, 8.0, ((0, 4), (1, 8))),
        "up_pre": normal_values(seeds[2], (TOKENS, FF), 1.0, 6.0, ((0, 4), (1, 8))),
        "down_weight": normal_values(seeds[3], (D, FF), D ** -0.5, 0.0625, ((1, 8),)),
        "block_scales": jnp.clip(jnp.exp(math.log(4.0) - 2.7725887 * jax.random.uniform(seeds[4], (D // 128, FF // 128), jnp.float32) ** level_of(seeds[4], (D // 128, FF // 128), ((1, 8),), -0.2, 0.2)), 0.25, 4.0).astype(jnp.bfloat16),
    }


def tile_quant(values, tile_axis):
    largest = jnp.max(jnp.abs(values), axis=tile_axis, keepdims=True)
    tile_scale = (largest + 1e-6) / 448.0
    payload = (values / tile_scale).astype(jnp.bfloat16)
    return (payload.astype(jnp.float32) * tile_scale).astype(jnp.bfloat16)


def reference(out_grad, gate_pre, up_pre, down_weight, block_scales):
    width = down_weight.shape[0]
    hidden_units = down_weight.shape[1]
    total = out_grad.shape[0]
    weight_deq = (down_weight.reshape(width // 128, 128, hidden_units // 128, 128)
                  * block_scales[:, None, :, None]).reshape(width, hidden_units).astype(jnp.bfloat16)
    grad_full = out_grad.astype(jnp.float32)
    grad_rowq = tile_quant(grad_full.reshape(total, width // 128, 128), 2).reshape(total, width)
    grad_colq = tile_quant(grad_full.reshape(total // 128, 128, width), 1).reshape(total, width)
    hidden_grad = jnp.dot(grad_rowq, weight_deq, preferred_element_type=jnp.float32)
    gate_val = gate_pre.astype(jnp.float32)
    up_val = up_pre.astype(jnp.float32)
    sigma = 1.0 / (1.0 + jnp.exp(-gate_val))
    gate_grad = (hidden_grad * up_val * sigma * (1.0 + gate_val * (1.0 - sigma))).astype(jnp.bfloat16)
    up_grad = (hidden_grad * gate_val * sigma).astype(jnp.bfloat16)
    hidden_val = gate_val * sigma * up_val
    hidden_colq = tile_quant(hidden_val.reshape(total // 128, 128, hidden_units), 1).reshape(total, hidden_units)
    grad_reps = grad_colq.reshape(N_DP, TOK, width)
    hidden_reps = hidden_colq.reshape(N_DP, TOK, hidden_units)

    def add_replica(running, pair):
        grad_block, hidden_block = pair
        term = lax.dot_general(grad_block, hidden_block, (((0,), (0,)), ((), ())),
                               preferred_element_type=jnp.float32)
        term = lax.optimization_barrier(term.astype(jnp.bfloat16)).astype(jnp.float32)
        return running + term, None

    summed, _ = lax.scan(add_replica, jnp.zeros((width, hidden_units), jnp.float32), (grad_reps, hidden_reps))
    return gate_grad, up_grad, summed.astype(jnp.bfloat16)
```

```python
import jax
import jax.numpy as jnp
from jax import lax
from jax.experimental import pallas as pl
from jax.experimental.pallas import tpu as pltpu
from jax.sharding import PartitionSpec as P

BF16 = jnp.bfloat16
F32 = jnp.float32
BOTH = ("dp", "tp")
TILE = 128


def tile_quant(values, tile_axis):
    largest = jnp.max(jnp.abs(values), axis=tile_axis, keepdims=True)
    tile_scale = (largest + 1e-06) / 448.0
    payload = (values / tile_scale).astype(jnp.bfloat16)
    return (payload.astype(jnp.float32) * tile_scale).astype(jnp.bfloat16)


def fast_quant(values, tile_axis):
    largest = jnp.max(jnp.abs(values), axis=tile_axis, keepdims=True)
    tile_scale = (largest + 1e-06) / 448.0
    payload = (values * (1.0 / tile_scale)).astype(BF16)
    return (payload.astype(F32) * tile_scale).astype(BF16)


def any_mesh(out_grad, gate_pre, up_pre, down_weight, block_scales):
    width = down_weight.shape[0]
    hidden_units = down_weight.shape[1]
    weight_deq = (
        down_weight.reshape(width // 128, 128, hidden_units // 128, 128)
        * block_scales[:, None, :, None]
    ).reshape(width, hidden_units)
    grad_tokens = lax.all_gather(out_grad, "tp", axis=0, tiled=True)
    local_tokens = grad_tokens.shape[0]
    grad_full = grad_tokens.astype(jnp.float32)
    grad_rowq = tile_quant(grad_full.reshape(local_tokens, width // 128, 128), 2).reshape(
        local_tokens, width
    )
    grad_colq = tile_quant(grad_full.reshape(local_tokens // 128, 128, width), 1).reshape(
        local_tokens, width
    )
    hidden_grad = jnp.dot(grad_rowq, weight_deq, preferred_element_type=jnp.float32)
    gate_val = gate_pre.astype(jnp.float32)
    up_val = up_pre.astype(jnp.float32)
    sigma = 1.0 / (1.0 + jnp.exp(-gate_val))
    gate_grad = (hidden_grad * up_val * sigma * (1.0 + gate_val * (1.0 - sigma))).astype(
        jnp.bfloat16
    )
    up_grad = (hidden_grad * gate_val * sigma).astype(jnp.bfloat16)
    hidden_val = gate_val * sigma * up_val
    hidden_colq = tile_quant(hidden_val.reshape(local_tokens // 128, 128, hidden_units), 1).reshape(
        local_tokens, hidden_units
    )
    width_dev = width // lax.axis_size("dp")
    every_cols = lax.all_to_all(grad_colq, "dp", split_axis=1, concat_axis=0, tiled=True)
    start_sum = jnp.zeros((width_dev, hidden_units), jnp.float32)
    hidden_piece = lax.all_gather(hidden_colq, "dp", axis=0, tiled=True)
    block_count = hidden_piece.shape[0] // local_tokens

    def one_block(block_num, inner):
        hidden_block = lax.dynamic_slice_in_dim(
            hidden_piece, block_num * local_tokens, local_tokens, 0
        )
        grad_block = lax.dynamic_slice_in_dim(every_cols, block_num * local_tokens, local_tokens, 0)
        term = lax.dot_general(
            grad_block, hidden_block, (((0,), (0,)), ((), ())), preferred_element_type=jnp.float32
        )
        term = lax.optimization_barrier(term.astype(jnp.bfloat16)).astype(jnp.float32)
        return inner + term

    summed = lax.fori_loop(0, block_count, one_block, start_sum)
    return (gate_grad, up_grad, summed.astype(jnp.bfloat16))


def whole(shape):
    return pl.BlockSpec(shape, lambda *_: (0,) * len(shape))


def split_columns(table, out_grad, parts):
    rows, width = out_grad.shape
    part = width // parts

    def body(table_ref, grad_ref, *outs):
        for j, out in enumerate(outs):
            start = pl.multiple_of((table_ref[0] ^ j) * part, TILE)
            out[...] = grad_ref[:, pl.ds(start, part)]

    return pl.pallas_call(
        body,
        name="split_columns",
        out_shape=[jax.ShapeDtypeStruct((rows, part), BF16)] * parts,
        grid_spec=pltpu.PrefetchScalarGridSpec(
            num_scalar_prefetch=1,
            grid=(1,),
            in_specs=[whole((rows, width))],
            out_specs=[whole((rows, part))] * parts,
        ),
    )(table, out_grad)


def hidden_quant(gate_pre, up_pre):
    tokens, units = gate_pre.shape
    block = units // 2 if units % 256 == 0 else units

    def body(gate_ref, up_ref, out_ref):
        gate = gate_ref[...].astype(F32)
        sigma = 1.0 / (1.0 + jnp.exp(-gate))
        out_ref[...] = fast_quant(gate * sigma * up_ref[...].astype(F32), 0)

    spec = pl.BlockSpec((tokens, block), lambda i: (0, i))
    return pl.pallas_call(
        body,
        name="hidden_quant",
        out_shape=jax.ShapeDtypeStruct((tokens, units), BF16),
        grid=(units // block,),
        in_specs=[spec, spec],
        out_specs=spec,
        cost_estimate=pl.CostEstimate(flops=20 * tokens * units, bytes_accessed=6 * tokens * units, transcendentals=tokens * units),
    )(gate_pre, up_pre)


def partial_hidden(table, pieces_p, pieces_q, down_weight, scales, step):
    count = len(pieces_p)
    rows2, part = pieces_p[0].shape
    rows = rows2 // 2
    units = down_weight.shape[1]
    total = 4 * count * rows
    each = count * rows

    def body(table_ref, scale_ref, *refs):
        p_refs, q_refs = refs[:count], refs[count : 2 * count]
        weight_ref = refs[2 * count]
        outs = refs[2 * count + 1 : 2 * count + 5]
        quant_ref = refs[2 * count + 5]
        at = pl.program_id(0)

        @pl.when(at == 0)
        def _():
            for half, group in enumerate((p_refs, q_refs)):
                for k, ref in enumerate(group):
                    for c in range(part // TILE):
                        cols = slice(c * TILE, (c + 1) * TILE)
                        deq = fast_quant(ref[:, cols].astype(F32), 1)
                        for s in range(2):
                            base = (2 * half + s) * each + k * rows
                            quant_ref[base : base + rows, cols] = deq[s * rows : (s + 1) * rows]

        row0 = table_ref[0] * (part // TILE)
        col0 = at * (step // TILE)
        blocks = []
        for a in range(part // TILE):
            line = []
            for b in range(step // TILE):
                scale = jnp.full((TILE, TILE), scale_ref[row0 + a, col0 + b], F32).astype(BF16)
                line.append(
                    weight_ref[a * TILE : (a + 1) * TILE, b * TILE : (b + 1) * TILE] * scale
                )
            blocks.append(jnp.concatenate(line, axis=1))
        weight = jnp.concatenate(blocks, axis=0)
        result = jnp.dot(quant_ref[...], weight, preferred_element_type=F32)
        for j, out in enumerate(outs):
            out[...] = result[j * each : (j + 1) * each].astype(out.dtype)

    return pl.pallas_call(
        body,
        name="partial_hidden",
        out_shape=[jax.ShapeDtypeStruct((each, units), BF16)] * 4,
        grid_spec=pltpu.PrefetchScalarGridSpec(
            num_scalar_prefetch=2,
            grid=(units // step,),
            in_specs=[whole((rows2, part))] * (2 * count)
            + [pl.BlockSpec((part, step), lambda i, tab, sc: (tab[0], i))],
            out_specs=[pl.BlockSpec((each, step), lambda i, tab, sc: (0, i))] * 4,
            scratch_shapes=[pltpu.VMEM((total, part), BF16)],
        ),
        compiler_params=pltpu.CompilerParams(vmem_limit_bytes=40 * 1024 * 1024),
        cost_estimate=pl.CostEstimate(flops=2 * total * part * units, bytes_accessed=2 * part * units, transcendentals=0),
    )(table, scales, *pieces_p, *pieces_q, down_weight)


def down_product(table, pieces_p, pieces_q, hiddens, step):
    count = len(pieces_p)
    rows2, part = pieces_p[0].shape
    rows = rows2 // 2
    tokens, units = hiddens[0].shape

    def body(table_ref, *refs):
        p_refs, q_refs = refs[:count], refs[count : 2 * count]
        h_refs = refs[2 * count : 2 * count + 4]
        out_ref = refs[2 * count + 4]
        hid_ref, quant_ref = refs[2 * count + 5 :]
        at = pl.program_id(0)

        @pl.when(at == 0)
        def _():
            for j, ref in enumerate(h_refs):
                hid_ref[j * tokens : (j + 1) * tokens, :] = ref[...]

        cols = pl.ds(pl.multiple_of(at * step, TILE), step)
        for j in range(4):
            group = (p_refs, q_refs)[j // 2]
            low = (j % 2) * rows
            vals = [ref[low : low + rows, cols].astype(F32) for ref in group]
            top = jnp.abs(vals[0])
            for v in vals[1:]:
                top = jnp.maximum(top, jnp.abs(v))
            scale = (jnp.max(top, axis=0, keepdims=True) + 1e-06) / 448.0
            inverse = 1.0 / scale
            for k, v in enumerate(vals):
                payload = (v * inverse).astype(BF16)
                start = pl.multiple_of(j * tokens + table_ref[1 + k], rows)
                quant_ref[pl.ds(start, rows), :] = (payload.astype(F32) * scale).astype(BF16)
        out_ref[...] = lax.dot_general(
            quant_ref[...], hid_ref[...], (((0,), (0,)), ((), ())), preferred_element_type=F32
        ).astype(BF16)

    return pl.pallas_call(
        body,
        name="down_product",
        out_shape=jax.ShapeDtypeStruct((part, units), BF16),
        grid_spec=pltpu.PrefetchScalarGridSpec(
            num_scalar_prefetch=1,
            grid=(part // step,),
            in_specs=[whole((rows2, part))] * (2 * count) + [whole((tokens, units))] * 4,
            out_specs=pl.BlockSpec((step, units), lambda i, tab: (i, 0)),
            scratch_shapes=[pltpu.VMEM((4 * tokens, units), BF16), pltpu.VMEM((4 * tokens, step), BF16)],
        ),
        compiler_params=pltpu.CompilerParams(vmem_limit_bytes=40 * 1024 * 1024),
        cost_estimate=pl.CostEstimate(flops=8 * part * tokens * units, bytes_accessed=2 * part * units, transcendentals=0),
    )(table, *pieces_p, *pieces_q, *hiddens)


def last_step(table, gate_pre, up_pre, groups):
    tokens, units = gate_pre.shape
    sizes = [len(g) for g in groups]
    flat = [a for g in groups for a in g]
    lengths = [g[0].shape[0] for g in groups]
    block = units // 2 if units % 256 == 0 else units

    def body(table_ref, gate_ref, up_ref, *refs):
        ins, (gate_out, up_out) = refs[:-2], refs[-2:]
        rows = tokens // (table.shape[0] - 1)
        at = piece = 0
        for size, length in zip(sizes, lengths):
            for first in range(0, length, rows):
                where = pl.ds(pl.multiple_of(table_ref[1 + piece], rows), rows)
                grad = ins[at][first : first + rows, :].astype(F32)
                for ref in ins[at + 1 : at + size]:
                    grad = grad + ref[first : first + rows, :].astype(F32)
                gate = gate_ref[where, :].astype(F32)
                up = up_ref[where, :].astype(F32)
                sigma = 1.0 / (1.0 + jnp.exp(-gate))
                gate_out[where, :] = (grad * up * sigma * (1.0 + gate * (1.0 - sigma))).astype(BF16)
                up_out[where, :] = (grad * gate * sigma).astype(BF16)
                piece += 1
            at += size

    spec = pl.BlockSpec((tokens, block), lambda i, tab: (0, i))
    return pl.pallas_call(
        body,
        name="last_step",
        out_shape=[jax.ShapeDtypeStruct((tokens, units), BF16)] * 2,
        grid_spec=pltpu.PrefetchScalarGridSpec(
            num_scalar_prefetch=1,
            grid=(units // block,),
            in_specs=[spec, spec]
            + [pl.BlockSpec((a.shape[0], block), lambda i, tab: (0, i)) for a in flat],
            out_specs=[spec, spec],
        ),
        cost_estimate=pl.CostEstimate(flops=20 * tokens * units, bytes_accessed=12 * tokens * units, transcendentals=tokens * units),
    )(table, gate_pre, up_pre, *flat)


def fold(own, received):
    return (own[0].astype(F32) + received[0].astype(F32)), (
        own[1].astype(F32) + received[1].astype(F32)
    ).astype(BF16)


def ring_place(index, count):
    return jnp.where(index % 2 == 0, index // 2, count - 1 - index // 2)


def ring_index(place, count):
    return jnp.where(place < count // 2, 2 * place, 2 * (count - 1 - place) + 1)


def pair_mesh(n_tp, out_grad, gate_pre, up_pre, down_weight, block_scales):
    rows = out_grad.shape[0]
    half = n_tp // 2
    order = [2 * i for i in range(half)] + [2 * (n_tp - 1 - i) + 1 for i in range(half, n_tp)]
    up = {order[i]: order[(i + 1) % n_tp] for i in range(n_tp)}
    down = {v: k for k, v in up.items()}

    def permute(value, target):
        pairs = []
        for d in range(4):
            for t in range(n_tp):
                dd, tt = target(d, t)
                pairs.append((d * n_tp + t, dd * n_tp + tt))
        return lax.ppermute(value, BOTH, pairs)

    def flip(value, bits):
        return permute(value, lambda d, t: (d ^ bits, t))

    def send_up(value):
        return permute(value, lambda d, t: (d, up[t]))

    def send_down(value):
        return permute(value, lambda d, t: (d, down[t]))

    offsets = [0]
    for k in range(1, half):
        offsets += [-k, k]
    offsets.append(half)
    place = ring_place(lax.axis_index("tp"), n_tp)
    sources = ring_index((place + jnp.array(offsets, jnp.int32)) % n_tp, n_tp)
    table = jnp.concatenate(
        [lax.axis_index("dp").reshape(1), sources * rows]
    ).astype(jnp.int32)
    scales = block_scales.astype(F32)

    parts = split_columns(table, out_grad, 4)
    from_core = flip(parts[1], 1)
    from_chip = flip(parts[2], 2)
    from_far = flip(parts[3], 3)
    hidden_own = hidden_quant(gate_pre, up_pre)
    block_p = jnp.concatenate([parts[0], from_core], axis=0)
    block_q = jnp.concatenate([from_chip, from_far], axis=0)

    pieces_p, pieces_q = {0: block_p}, {0: block_q}
    for k in range(1, half + 1):
        pieces_p[-k] = send_up(pieces_p[1 - k])
        if k < half:
            pieces_p[k] = send_down(pieces_p[k - 1])
            pieces_q[-k] = send_up(pieces_q[1 - k])
        pieces_q[k] = send_down(pieces_q[k - 1])
    pieces_p[half] = pieces_p[-half]
    list_p = [pieces_p[o] for o in offsets]
    list_q = [pieces_q[o] for o in offsets]

    hidden_chip = flip(hidden_own, 2)
    hidden_core = flip(hidden_own, 1)
    hidden_far = flip(hidden_chip, 1)

    first = n_tp - 3
    groups = []
    part1 = partial_hidden(table, list_p[:first], list_q[:first], down_weight, scales, 256)
    got0, got2 = flip(part1[1], 1), flip(part1[3], 1)
    sum0, sum2 = fold((part1[0], part1[2]), (got0, got2))
    groups.append([sum0, flip(sum2, 2)])
    part2 = partial_hidden(table, list_p[first:], list_q[first:], down_weight, scales, 256)
    groups.append([part2[0]] + [flip(part2[j], j) for j in (1, 2, 3)])
    down_grad = down_product(
        table, list_p, list_q, [hidden_own, hidden_core, hidden_chip, hidden_far], 256
    )
    gate_grad, up_grad = last_step(table, gate_pre, up_pre, groups)
    return gate_grad, up_grad, down_grad


def solution(mesh):
    n_dp, n_tp = mesh.shape["dp"], mesh.shape["tp"]

    def per_device(out_grad, gate_pre, up_pre, down_weight, block_scales):
        part = down_weight.shape[0] // n_dp
        rows = out_grad.shape[0]
        fits = (
            n_dp == 4
            and n_tp >= 4
            and n_tp % 2 == 0
            and rows % 16 == 0
            and rows * n_tp == 128
            and part % 256 == 0
            and gate_pre.shape[1] % 256 == 0
        )
        if fits:
            return pair_mesh(n_tp, out_grad, gate_pre, up_pre, down_weight, block_scales)
        return any_mesh(out_grad, gate_pre, up_pre, down_weight, block_scales)

    placed = (P(("dp", "tp"), None), P("dp", "tp"), P("dp", "tp"), P(None, "tp"), P(None, "tp"))
    return jax.shard_map(
        per_device,
        mesh=mesh,
        in_specs=placed,
        out_specs=(P("dp", "tp"), P("dp", "tp"), P("dp", "tp")),
        check_vma=False,
    )
```

```python
import jax
import jax.numpy as jnp
from jax import lax
from jax.experimental import pallas as pl
from jax.experimental.pallas import tpu as pltpu
from jax.sharding import PartitionSpec as P

BF16 = jnp.bfloat16
F32 = jnp.float32
BOTH = ("dp", "tp")
TILE = 128


def tile_quant(values, tile_axis):
    largest = jnp.max(jnp.abs(values), axis=tile_axis, keepdims=True)
    tile_scale = (largest + 1e-06) / 448.0
    payload = (values / tile_scale).astype(jnp.bfloat16)
    return (payload.astype(jnp.float32) * tile_scale).astype(jnp.bfloat16)


def fast_quant(values, tile_axis):
    largest = jnp.max(jnp.abs(values), axis=tile_axis, keepdims=True)
    tile_scale = (largest + 1e-06) / 448.0
    payload = (values * (1.0 / tile_scale)).astype(BF16)
    return (payload.astype(F32) * tile_scale).astype(BF16)


def any_mesh(out_grad, gate_pre, up_pre, down_weight, block_scales):
    width = down_weight.shape[0]
    hidden_units = down_weight.shape[1]
    weight_deq = (
        down_weight.reshape(width // 128, 128, hidden_units // 128, 128)
        * block_scales[:, None, :, None]
    ).reshape(width, hidden_units)
    grad_tokens = lax.all_gather(out_grad, "tp", axis=0, tiled=True)
    local_tokens = grad_tokens.shape[0]
    grad_full = grad_tokens.astype(jnp.float32)
    grad_rowq = tile_quant(grad_full.reshape(local_tokens, width // 128, 128), 2).reshape(
        local_tokens, width
    )
    grad_colq = tile_quant(grad_full.reshape(local_tokens // 128, 128, width), 1).reshape(
        local_tokens, width
    )
    hidden_grad = jnp.dot(grad_rowq, weight_deq, preferred_element_type=jnp.float32)
    gate_val = gate_pre.astype(jnp.float32)
    up_val = up_pre.astype(jnp.float32)
    sigma = 1.0 / (1.0 + jnp.exp(-gate_val))
    gate_grad = (hidden_grad * up_val * sigma * (1.0 + gate_val * (1.0 - sigma))).astype(
        jnp.bfloat16
    )
    up_grad = (hidden_grad * gate_val * sigma).astype(jnp.bfloat16)
    hidden_val = gate_val * sigma * up_val
    hidden_colq = tile_quant(hidden_val.reshape(local_tokens // 128, 128, hidden_units), 1).reshape(
        local_tokens, hidden_units
    )
    width_dev = width // lax.axis_size("dp")
    every_cols = lax.all_to_all(grad_colq, "dp", split_axis=1, concat_axis=0, tiled=True)
    start_sum = jnp.zeros((width_dev, hidden_units), jnp.float32)
    hidden_piece = lax.all_gather(hidden_colq, "dp", axis=0, tiled=True)
    block_count = hidden_piece.shape[0] // local_tokens

    def one_block(block_num, inner):
        hidden_block = lax.dynamic_slice_in_dim(
            hidden_piece, block_num * local_tokens, local_tokens, 0
        )
        grad_block = lax.dynamic_slice_in_dim(every_cols, block_num * local_tokens, local_tokens, 0)
        term = lax.dot_general(
            grad_block, hidden_block, (((0,), (0,)), ((), ())), preferred_element_type=jnp.float32
        )
        term = lax.optimization_barrier(term.astype(jnp.bfloat16)).astype(jnp.float32)
        return inner + term

    summed = lax.fori_loop(0, block_count, one_block, start_sum)
    return (gate_grad, up_grad, summed.astype(jnp.bfloat16))


VMEM = pl.BlockSpec(memory_space=pltpu.VMEM)
SMEM = pl.BlockSpec(memory_space=pltpu.SMEM)
HBM = pl.BlockSpec(memory_space=pltpu.HBM)
MIB = 1024 * 1024


def like(*shape, dtype=BF16):
    return jax.ShapeDtypeStruct(shape, dtype)


def ring_sources(n_tp, offsets):
    half = n_tp // 2
    me = lax.axis_index("tp")
    odd = lax.rem(me, 2)
    place = jnp.where(odd == 1, n_tp - 1 - me // 2, me // 2)
    result = []
    for offset in offsets:
        at = lax.rem(place + offset + n_tp, n_tp)
        result.append(jnp.where(at < half, 2 * at, 2 * (n_tp - 1 - at) + 1))
    return result


def split_columns(out_grad, parts):
    rows, width = out_grad.shape
    part = width // parts

    def body(grad_ref, *refs):
        outs, sems = refs[:parts], refs[parts]
        me = lax.axis_index("dp")
        copies = []
        for j in range(parts):
            start = pl.multiple_of((me ^ j) * part, TILE)
            copies.append(
                pltpu.make_async_copy(grad_ref.at[:, pl.ds(start, part)], outs[j], sems.at[j])
            )
            copies[-1].start()
        for copy in copies:
            copy.wait()

    return pl.pallas_call(
        body,
        name="split_columns",
        out_shape=[like(rows, part)] * parts,
        in_specs=[HBM],
        out_specs=[VMEM] * parts,
        scratch_shapes=[pltpu.SemaphoreType.DMA((parts,))],
    )(out_grad)


def hidden_quant(gate_pre, up_pre):
    tokens, units = gate_pre.shape

    def body(gate_ref, up_ref, hidden_ref, gate_factor, up_factor):
        for c in range(units // TILE):
            at = (slice(None), slice(c * TILE, (c + 1) * TILE))
            gate = gate_ref[at].astype(F32)
            up = up_ref[at].astype(F32)
            sigma = 1.0 / (1.0 + jnp.exp(-gate))
            hidden_ref[at] = fast_quant(gate * sigma * up, 0)
            gate_factor[at] = up * sigma * (1.0 + gate * (1.0 - sigma))
            up_factor[at] = gate * sigma

    return pl.pallas_call(
        body,
        name="hidden_quant",
        out_shape=[like(tokens, units)] + [like(tokens, units, dtype=F32)] * 2,
        in_specs=[VMEM] * 2,
        out_specs=[VMEM] * 3,
        compiler_params=pltpu.CompilerParams(vmem_limit_bytes=16 * MIB),
        cost_estimate=pl.CostEstimate(
            flops=20 * tokens * units, bytes_accessed=14 * tokens * units, transcendentals=tokens * units
        ),
    )(gate_pre, up_pre)


def weight_rows(down_weight, scales, parts):
    width, units = down_weight.shape
    part = width // parts
    chunk = 2 * TILE
    count = part // chunk

    def body(scale_ref, weight_ref, out_ref, sems):
        me = lax.axis_index("dp")
        copies = []
        for i in range(count):
            start = pl.multiple_of(me * part + i * chunk, TILE)
            copies.append(
                pltpu.make_async_copy(
                    weight_ref.at[pl.ds(start, chunk)],
                    out_ref.at[pl.ds(i * chunk, chunk)],
                    sems.at[i],
                )
            )
            copies[-1].start()
        row0 = me * (part // TILE)
        for i in range(count):
            copies[i].wait()
            for a in range(i * chunk // TILE, (i + 1) * chunk // TILE):
                for b in range(units // TILE):
                    at = (slice(a * TILE, (a + 1) * TILE), slice(b * TILE, (b + 1) * TILE))
                    scale = jnp.full((TILE, TILE), scale_ref[row0 + a, b], F32).astype(BF16)
                    out_ref[at] = out_ref[at] * scale

    return pl.pallas_call(
        body,
        name="weight_rows",
        out_shape=like(part, units),
        in_specs=[SMEM, HBM],
        out_specs=VMEM,
        scratch_shapes=[pltpu.SemaphoreType.DMA((count,))],
        compiler_params=pltpu.CompilerParams(vmem_limit_bytes=48 * MIB),
        cost_estimate=pl.CostEstimate(flops=part * units, bytes_accessed=4 * part * units, transcendentals=0),
    )(scales, down_weight)


def partial_hidden(pieces_p, pieces_q, weight):
    count = len(pieces_p)
    rows2, part = pieces_p[0].shape
    rows = rows2 // 2
    units = weight.shape[1]
    each = count * rows
    step = 512 if units % 512 == 0 else 256

    def body(*refs):
        groups = refs[:count], refs[count : 2 * count]
        weight_ref = refs[2 * count]
        outs = refs[2 * count + 1 : 2 * count + 5]
        quant_ref = refs[2 * count + 5]
        for half, group in enumerate(groups):
            for k, ref in enumerate(group):
                for c in range(part // TILE):
                    cols = slice(c * TILE, (c + 1) * TILE)
                    deq = fast_quant(ref[:, cols].astype(F32), 1)
                    for s in range(2):
                        base = (2 * half + s) * each + k * rows
                        quant_ref[base : base + rows, cols] = deq[s * rows : (s + 1) * rows]
        for i in range(units // step):
            cols = slice(i * step, (i + 1) * step)
            result = jnp.dot(quant_ref[...], weight_ref[:, cols], preferred_element_type=F32)
            for j, out in enumerate(outs):
                out[:, cols] = result[j * each : (j + 1) * each].astype(BF16)

    return pl.pallas_call(
        body,
        name="partial_hidden",
        out_shape=[like(each, units)] * 4,
        in_specs=[VMEM] * (2 * count + 1),
        out_specs=[VMEM] * 4,
        scratch_shapes=[pltpu.VMEM((4 * each, part), BF16)],
        compiler_params=pltpu.CompilerParams(vmem_limit_bytes=24 * MIB),
        cost_estimate=pl.CostEstimate(
            flops=8 * each * part * units, bytes_accessed=2 * part * units, transcendentals=0
        ),
    )(*pieces_p, *pieces_q, weight)


def down_product(n_tp, offsets, pieces_p, pieces_q, hiddens):
    count = len(pieces_p)
    rows2, part = pieces_p[0].shape
    rows = rows2 // 2
    tokens, units = hiddens[0].shape
    step, slots, split = 256, 3, 4
    steps = part // step

    def body(*refs):
        groups = refs[:count], refs[count : 2 * count]
        h_refs = refs[2 * count : 2 * count + 4]
        out_ref, token_ref, hid_ref, quant_ref, buffer, sems = refs[2 * count + 4 :]
        token_ref[...] = jnp.zeros(token_ref.shape, F32)
        starts = [pl.multiple_of(s * rows, rows) for s in ring_sources(n_tp, offsets)]
        for j, ref in enumerate(h_refs):
            for k, start in enumerate(starts):
                low = j * tokens + k * rows
                hid_ref[low : low + rows, :] = ref[pl.ds(start, rows), :]

        def copies(i):
            lines = step // split
            return [
                pltpu.make_async_copy(
                    buffer.at[i % slots, pl.ds(k * lines, lines)],
                    out_ref.at[pl.ds(i * step + k * lines, lines)],
                    sems.at[i % slots, k],
                )
                for k in range(split)
            ]

        for i in range(steps):
            if i >= slots:
                for copy in copies(i - slots):
                    copy.wait()
            for c in range(step // TILE):
                cols = slice(i * step + c * TILE, i * step + (c + 1) * TILE)
                for j in range(4):
                    low = (j % 2) * rows
                    vals = [ref[low : low + rows, cols].astype(F32) for ref in groups[j // 2]]
                    top = jnp.abs(vals[0])
                    for v in vals[1:]:
                        top = jnp.maximum(top, jnp.abs(v))
                    scale = (jnp.max(top, axis=0, keepdims=True) + 1e-06) / 448.0
                    inverse = 1.0 / scale
                    for k, v in enumerate(vals):
                        payload = (v * inverse).astype(BF16).astype(F32)
                        base = j * tokens + k * rows
                        quant_ref[base : base + rows, c * TILE : (c + 1) * TILE] = (
                            payload * scale
                        ).astype(BF16)
            buffer[i % slots] = lax.dot_general(
                quant_ref[...], hid_ref[...], (((0,), (0,)), ((), ())), preferred_element_type=F32
            ).astype(BF16)
            for copy in copies(i):
                copy.start()
        for i in range(max(0, steps - slots), steps):
            for copy in copies(i):
                copy.wait()

    return pl.pallas_call(
        body,
        name="down_product",
        out_shape=[like(part, units), like(8, TILE, dtype=F32)],
        in_specs=[VMEM] * (2 * count + 4),
        out_specs=[HBM, VMEM],
        scratch_shapes=[
            pltpu.VMEM((4 * tokens, units), BF16),
            pltpu.VMEM((4 * tokens, step), BF16),
            pltpu.VMEM((slots, step, units), BF16),
            pltpu.SemaphoreType.DMA((slots, split)),
        ],
        compiler_params=pltpu.CompilerParams(vmem_limit_bytes=24 * MIB),
        cost_estimate=pl.CostEstimate(
            flops=8 * part * tokens * units, bytes_accessed=2 * part * units, transcendentals=0
        ),
    )(*pieces_p, *pieces_q, *hiddens)


def last_step(n_tp, offsets, gate_factor, up_factor, groups, after):
    tokens, units = gate_factor.shape
    sizes = [len(g) for g in groups]
    lengths = [g[0].shape[0] for g in groups]
    flat = [a for g in groups for a in g]
    rows = tokens // len(offsets)
    split = 2
    half = units // split

    def body(gate_ref, up_ref, _, *refs):
        ins = refs[: len(flat)]
        gate_out, up_out, gate_buf, up_buf, sems = refs[len(flat) :]
        starts = [pl.multiple_of(s * rows, rows) for s in ring_sources(n_tp, offsets)]
        copies = []
        for h in range(split):
            cols = slice(h * half, (h + 1) * half)
            at = piece = 0
            for size, length in zip(sizes, lengths):
                for first in range(0, length, rows):
                    where = pl.ds(starts[piece], rows)
                    grad = ins[at][first : first + rows, cols].astype(F32)
                    for ref in ins[at + 1 : at + size]:
                        grad = grad + ref[first : first + rows, cols].astype(F32)
                    gate_buf[where, cols] = (grad * gate_ref[where, cols]).astype(BF16)
                    up_buf[where, cols] = (grad * up_ref[where, cols]).astype(BF16)
                    piece += 1
                at += size
            for k, (buf, out) in enumerate(((gate_buf, gate_out), (up_buf, up_out))):
                copies.append(
                    pltpu.make_async_copy(buf.at[:, cols], out.at[:, cols], sems.at[k, h])
                )
                copies[-1].start()
        for copy in copies:
            copy.wait()

    return pl.pallas_call(
        body,
        name="last_step",
        out_shape=[like(tokens, units)] * 2,
        in_specs=[VMEM] * (3 + len(flat)),
        out_specs=[HBM] * 2,
        scratch_shapes=[pltpu.VMEM((tokens, units), BF16)] * 2
        + [pltpu.SemaphoreType.DMA((2, split))],
        compiler_params=pltpu.CompilerParams(vmem_limit_bytes=16 * MIB),
        cost_estimate=pl.CostEstimate(
            flops=8 * tokens * units, bytes_accessed=16 * tokens * units, transcendentals=0
        ),
    )(gate_factor, up_factor, after, *flat)


def fold(own, received):
    return (own[0].astype(F32) + received[0].astype(F32)), (
        own[1].astype(F32) + received[1].astype(F32)
    ).astype(BF16)


def pair_mesh(n_tp, out_grad, gate_pre, up_pre, down_weight, block_scales):
    half = n_tp // 2
    order = [2 * i for i in range(half)] + [2 * (n_tp - 1 - i) + 1 for i in range(half, n_tp)]
    up = {order[i]: order[(i + 1) % n_tp] for i in range(n_tp)}
    down = {v: k for k, v in up.items()}

    def permute(value, target):
        pairs = []
        for d in range(4):
            for t in range(n_tp):
                dd, tt = target(d, t)
                pairs.append((d * n_tp + t, dd * n_tp + tt))
        return lax.ppermute(value, BOTH, pairs)

    def flip(value, bits):
        return permute(value, lambda d, t: (d ^ bits, t))

    def send_up(value):
        return permute(value, lambda d, t: (d, up[t]))

    def send_down(value):
        return permute(value, lambda d, t: (d, down[t]))

    offsets = [0]
    for k in range(1, half):
        offsets += [-k, k]
    offsets.append(half)

    parts = split_columns(out_grad, 4)
    from_core = flip(parts[1], 1)
    from_chip = flip(parts[2], 2)
    from_far = flip(parts[3], 3)
    hidden_own, gate_factor, up_factor = hidden_quant(gate_pre, up_pre)
    weight = weight_rows(down_weight, block_scales.astype(F32), 4)
    block_p = jnp.concatenate([parts[0], from_core], axis=0)
    block_q = jnp.concatenate([from_chip, from_far], axis=0)

    pieces_p, pieces_q = {0: block_p}, {0: block_q}
    for k in range(1, half + 1):
        pieces_p[-k] = send_up(pieces_p[1 - k])
        if k < half:
            pieces_p[k] = send_down(pieces_p[k - 1])
            pieces_q[-k] = send_up(pieces_q[1 - k])
        pieces_q[k] = send_down(pieces_q[k - 1])
    pieces_p[half] = pieces_p[-half]
    list_p = [pieces_p[o] for o in offsets]
    list_q = [pieces_q[o] for o in offsets]

    hidden_chip = flip(hidden_own, 2)
    hidden_core = flip(hidden_own, 1)
    hidden_far = flip(hidden_chip, 1)

    first = n_tp - 3
    groups = []
    part1 = partial_hidden(list_p[:first], list_q[:first], weight)
    got0, got2 = flip(part1[1], 1), flip(part1[3], 1)
    sum0, sum2 = fold((part1[0], part1[2]), (got0, got2))
    groups.append([sum0, flip(sum2, 2)])
    part2 = partial_hidden(list_p[first:], list_q[first:], weight)
    groups.append([part2[0]] + [flip(part2[j], j) for j in (1, 2, 3)])
    down_grad, token = down_product(
        n_tp, offsets, list_p, list_q, [hidden_own, hidden_core, hidden_chip, hidden_far]
    )
    gate_grad, up_grad = last_step(n_tp, offsets, gate_factor, up_factor, groups, token)
    return gate_grad, up_grad, down_grad


def solution(mesh):
    n_dp, n_tp = mesh.shape["dp"], mesh.shape["tp"]

    def per_device(out_grad, gate_pre, up_pre, down_weight, block_scales):
        part = down_weight.shape[0] // n_dp
        rows = out_grad.shape[0]
        fits = (
            n_dp == 4
            and n_tp >= 4
            and n_tp % 2 == 0
            and rows % 16 == 0
            and rows * n_tp == 128
            and part % 256 == 0
            and gate_pre.shape[1] % 256 == 0
        )
        if fits:
            return pair_mesh(n_tp, out_grad, gate_pre, up_pre, down_weight, block_scales)
        return any_mesh(out_grad, gate_pre, up_pre, down_weight, block_scales)

    placed = (P(("dp", "tp"), None), P("dp", "tp"), P("dp", "tp"), P(None, "tp"), P(None, "tp"))
    return jax.shard_map(
        per_device,
        mesh=mesh,
        in_specs=placed,
        out_specs=(P("dp", "tp"), P("dp", "tp"), P("dp", "tp")),
        check_vma=False,
    )
```

```python
import jax
import jax.numpy as jnp
from jax import lax
from jax.experimental import pallas as pl
from jax.experimental.pallas import tpu as pltpu
from jax.sharding import PartitionSpec as P

BF16 = jnp.bfloat16
F32 = jnp.float32
BOTH = ("dp", "tp")
TILE = 128


def tile_quant(values, tile_axis):
    largest = jnp.max(jnp.abs(values), axis=tile_axis, keepdims=True)
    tile_scale = (largest + 1e-06) / 448.0
    payload = (values / tile_scale).astype(jnp.bfloat16)
    return (payload.astype(jnp.float32) * tile_scale).astype(jnp.bfloat16)


def fast_quant(values, tile_axis):
    largest = jnp.max(jnp.abs(values), axis=tile_axis, keepdims=True)
    tile_scale = (largest + 1e-06) / 448.0
    payload = (values * (1.0 / tile_scale)).astype(BF16)
    return (payload.astype(F32) * tile_scale).astype(BF16)


def any_mesh(out_grad, gate_pre, up_pre, down_weight, block_scales):
    width = down_weight.shape[0]
    hidden_units = down_weight.shape[1]
    weight_deq = (
        down_weight.reshape(width // 128, 128, hidden_units // 128, 128)
        * block_scales[:, None, :, None]
    ).reshape(width, hidden_units)
    grad_tokens = lax.all_gather(out_grad, "tp", axis=0, tiled=True)
    local_tokens = grad_tokens.shape[0]
    grad_full = grad_tokens.astype(jnp.float32)
    grad_rowq = tile_quant(grad_full.reshape(local_tokens, width // 128, 128), 2).reshape(
        local_tokens, width
    )
    grad_colq = tile_quant(grad_full.reshape(local_tokens // 128, 128, width), 1).reshape(
        local_tokens, width
    )
    hidden_grad = jnp.dot(grad_rowq, weight_deq, preferred_element_type=jnp.float32)
    gate_val = gate_pre.astype(jnp.float32)
    up_val = up_pre.astype(jnp.float32)
    sigma = 1.0 / (1.0 + jnp.exp(-gate_val))
    gate_grad = (hidden_grad * up_val * sigma * (1.0 + gate_val * (1.0 - sigma))).astype(
        jnp.bfloat16
    )
    up_grad = (hidden_grad * gate_val * sigma).astype(jnp.bfloat16)
    hidden_val = gate_val * sigma * up_val
    hidden_colq = tile_quant(hidden_val.reshape(local_tokens // 128, 128, hidden_units), 1).reshape(
        local_tokens, hidden_units
    )
    width_dev = width // lax.axis_size("dp")
    every_cols = lax.all_to_all(grad_colq, "dp", split_axis=1, concat_axis=0, tiled=True)
    start_sum = jnp.zeros((width_dev, hidden_units), jnp.float32)
    hidden_piece = lax.all_gather(hidden_colq, "dp", axis=0, tiled=True)
    block_count = hidden_piece.shape[0] // local_tokens

    def one_block(block_num, inner):
        hidden_block = lax.dynamic_slice_in_dim(
            hidden_piece, block_num * local_tokens, local_tokens, 0
        )
        grad_block = lax.dynamic_slice_in_dim(every_cols, block_num * local_tokens, local_tokens, 0)
        term = lax.dot_general(
            grad_block, hidden_block, (((0,), (0,)), ((), ())), preferred_element_type=jnp.float32
        )
        term = lax.optimization_barrier(term.astype(jnp.bfloat16)).astype(jnp.float32)
        return inner + term

    summed = lax.fori_loop(0, block_count, one_block, start_sum)
    return (gate_grad, up_grad, summed.astype(jnp.bfloat16))


VMEM = pl.BlockSpec(memory_space=pltpu.VMEM)
SMEM = pl.BlockSpec(memory_space=pltpu.SMEM)
HBM = pl.BlockSpec(memory_space=pltpu.HBM)
MIB = 1024 * 1024


def like(*shape, dtype=BF16):
    return jax.ShapeDtypeStruct(shape, dtype)


def ring_sources(n_tp, offsets):
    half = n_tp // 2
    me = lax.axis_index("tp")
    odd = lax.rem(me, 2)
    place = jnp.where(odd == 1, n_tp - 1 - me // 2, me // 2)
    result = []
    for offset in offsets:
        at = lax.rem(place + offset + n_tp, n_tp)
        result.append(jnp.where(at < half, 2 * at, 2 * (n_tp - 1 - at) + 1))
    return result


def split_columns(out_grad, gate_pre, up_pre, parts):
    rows, width = out_grad.shape
    part = width // parts

    def body(grad_ref, gate_ref, up_ref, own, other, send, gate_out, up_out, sems):
        me = lax.axis_index("dp")
        pairs = [
            (grad_ref.at[:, pl.ds(pl.multiple_of((me ^ flips) * part, TILE), part)], target)
            for flips, target in (
                (2, send.at[pl.ds(0, rows)]),
                (3, send.at[pl.ds(rows, rows)]),
                (0, own),
                (1, other),
            )
        ]
        pairs += [(gate_ref, gate_out), (up_ref, up_out)]
        copies = [
            pltpu.make_async_copy(source, target, sems.at[i])
            for i, (source, target) in enumerate(pairs)
        ]
        for copy in copies:
            copy.start()
        for copy in copies:
            copy.wait()

    return pl.pallas_call(
        body,
        name="split_columns",
        out_shape=[pltpu.VMEM((rows, part), BF16)] * 2
        + [pltpu.VMEM((2 * rows, part), BF16)]
        + [pltpu.VMEM(gate_pre.shape, BF16)] * 2,
        in_specs=[HBM] * 3,
        out_specs=[VMEM] * 5,
        scratch_shapes=[pltpu.SemaphoreType.DMA((6,))],
    )(out_grad, gate_pre, up_pre)


def hidden_quant(gate_pre, up_pre):
    tokens, units = gate_pre.shape

    def body(gate_ref, up_ref, hidden_ref, gate_factor, up_factor):
        for c in range(units // TILE):
            at = (slice(None), slice(c * TILE, (c + 1) * TILE))
            gate = gate_ref[at].astype(F32)
            up = up_ref[at].astype(F32)
            sigma = 1.0 / (1.0 + jnp.exp(-gate))
            hidden_ref[at] = fast_quant(gate * sigma * up, 0)
            gate_factor[at] = up * sigma * (1.0 + gate * (1.0 - sigma))
            up_factor[at] = gate * sigma

    return pl.pallas_call(
        body,
        name="hidden_quant",
        out_shape=[like(tokens, units)] + [like(tokens, units, dtype=F32)] * 2,
        in_specs=[VMEM] * 2,
        out_specs=[VMEM] * 3,
        compiler_params=pltpu.CompilerParams(vmem_limit_bytes=16 * MIB),
        cost_estimate=pl.CostEstimate(
            flops=20 * tokens * units, bytes_accessed=14 * tokens * units, transcendentals=tokens * units
        ),
    )(gate_pre, up_pre)


def weight_rows(down_weight, scales, parts, flips):
    width, units = down_weight.shape
    part = width // parts
    chunk = 2 * TILE
    count = part // chunk

    def body(scale_ref, weight_ref, out_ref, sems):
        me = lax.axis_index("dp") ^ flips
        copies = []
        for i in range(count):
            start = pl.multiple_of(me * part + i * chunk, TILE)
            copies.append(
                pltpu.make_async_copy(
                    weight_ref.at[pl.ds(start, chunk)],
                    out_ref.at[pl.ds(i * chunk, chunk)],
                    sems.at[i],
                )
            )
            copies[-1].start()
        row0 = me * (part // TILE)
        for i in range(count):
            copies[i].wait()
            for a in range(i * chunk // TILE, (i + 1) * chunk // TILE):
                for b in range(units // TILE):
                    at = (slice(a * TILE, (a + 1) * TILE), slice(b * TILE, (b + 1) * TILE))
                    scale = jnp.full((TILE, TILE), scale_ref[row0 + a, b], F32).astype(BF16)
                    out_ref[at] = out_ref[at] * scale

    return pl.pallas_call(
        body,
        name="weight_rows",
        out_shape=like(part, units),
        in_specs=[SMEM, HBM],
        out_specs=VMEM,
        scratch_shapes=[pltpu.SemaphoreType.DMA((count,))],
        compiler_params=pltpu.CompilerParams(vmem_limit_bytes=44 * MIB),
        cost_estimate=pl.CostEstimate(flops=part * units, bytes_accessed=4 * part * units, transcendentals=0),
    )(scales, down_weight)


def grouped(refs, sizes):
    result, at = [], 0
    for size in sizes:
        result.append(refs[at : at + size])
        at += size
    return result


def half_of(piece, h):
    return (piece[0], h * piece[0].shape[0] // 2) if len(piece) == 1 else (piece[h], 0)


def partial_hidden(rows, pieces, weights):
    sizes = [len(p) for p in pieces]
    flat = [a for p in pieces for a in p]
    part, units = weights[0].shape
    each = len(pieces) * rows
    step = 512 if units % 512 == 0 else 256

    def body(*refs):
        first_ref, second_ref, keep_ref, send_ref, quant_ref = refs[len(flat) :]
        for k, piece in enumerate(grouped(refs, sizes)):
            for h in range(2):
                ref, low = half_of(piece, h)
                for c in range(part // TILE):
                    cols = slice(c * TILE, (c + 1) * TILE)
                    deq = fast_quant(ref[low : low + 2 * rows, cols].astype(F32), 1)
                    into = slice(h * part + c * TILE, h * part + (c + 1) * TILE)
                    for s in range(2):
                        base = s * each + k * rows
                        quant_ref[base : base + rows, into] = deq[s * rows : (s + 1) * rows]
        for i in range(units // step):
            cols = slice(i * step, (i + 1) * step)
            result = jnp.dot(quant_ref[:, :part], first_ref[:, cols], preferred_element_type=F32)
            result += jnp.dot(quant_ref[:, part:], second_ref[:, cols], preferred_element_type=F32)
            keep_ref[:, cols] = result[:each].astype(keep_ref.dtype)
            send_ref[:, cols] = result[each:].astype(BF16)

    return pl.pallas_call(
        body,
        name="partial_hidden",
        out_shape=[like(each, units, dtype=F32), like(each, units)],
        in_specs=[VMEM] * (len(flat) + 2),
        out_specs=[VMEM] * 2,
        scratch_shapes=[pltpu.VMEM((2 * each, 2 * part), BF16)],
        compiler_params=pltpu.CompilerParams(vmem_limit_bytes=16 * MIB),
        cost_estimate=pl.CostEstimate(
            flops=8 * each * part * units, bytes_accessed=4 * part * units, transcendentals=0
        ),
    )(*flat, *weights)


def down_product(n_tp, offsets, pieces, others, hiddens):
    flat = [p[0] for p in pieces] + list(others)
    part = flat[0].shape[1]
    tokens, units = hiddens[0].shape
    rows = tokens // len(pieces)
    step, slots, split = 256, 3, 4
    steps = part // step

    def body(*refs):
        own, other = refs[: len(pieces)], refs[len(pieces) : len(flat)]
        where = [[(ref, s * rows) for ref in own] for s in range(2)]
        where += [
            [(ref, low + s * rows) for ref in other for low in range(0, ref.shape[0], 2 * rows)]
            for s in range(2)
        ]
        h_refs = refs[len(flat) : len(flat) + 4]
        out_ref, token_ref, hid_ref, quant_ref, buffer, sems = refs[len(flat) + 4 :]
        token_ref[...] = jnp.zeros(token_ref.shape, F32)
        starts = [pl.multiple_of(s * rows, rows) for s in ring_sources(n_tp, offsets)]
        for j, ref in enumerate(h_refs):
            for k, start in enumerate(starts):
                low = j * tokens + k * rows
                hid_ref[low : low + rows, :] = ref[pl.ds(start, rows), :]

        def copies(i):
            lines = step // split
            return [
                pltpu.make_async_copy(
                    buffer.at[i % slots, pl.ds(k * lines, lines)],
                    out_ref.at[pl.ds(i * step + k * lines, lines)],
                    sems.at[i % slots, k],
                )
                for k in range(split)
            ]

        for i in range(steps):
            if i >= slots:
                for copy in copies(i - slots):
                    copy.wait()
            for c in range(step // TILE):
                cols = slice(i * step + c * TILE, i * step + (c + 1) * TILE)
                for j in range(4):
                    vals = [ref[low : low + rows, cols].astype(F32) for ref, low in where[j]]
                    top = jnp.abs(vals[0])
                    for v in vals[1:]:
                        top = jnp.maximum(top, jnp.abs(v))
                    scale = (jnp.max(top, axis=0, keepdims=True) + 1e-06) / 448.0
                    inverse = 1.0 / scale
                    for k, v in enumerate(vals):
                        payload = (v * inverse).astype(BF16).astype(F32)
                        base = j * tokens + k * rows
                        quant_ref[base : base + rows, c * TILE : (c + 1) * TILE] = (
                            payload * scale
                        ).astype(BF16)
            buffer[i % slots] = lax.dot_general(
                quant_ref[...], hid_ref[...], (((0,), (0,)), ((), ())), preferred_element_type=F32
            ).astype(BF16)
            for copy in copies(i):
                copy.start()
        for i in range(max(0, steps - slots), steps):
            for copy in copies(i):
                copy.wait()

    return pl.pallas_call(
        body,
        name="down_product",
        out_shape=[like(part, units), like(8, TILE, dtype=F32)],
        in_specs=[VMEM] * (len(flat) + 4),
        out_specs=[HBM, VMEM],
        scratch_shapes=[
            pltpu.VMEM((4 * tokens, units), BF16),
            pltpu.VMEM((4 * tokens, step), BF16),
            pltpu.VMEM((slots, step, units), BF16),
            pltpu.SemaphoreType.DMA((slots, split)),
        ],
        compiler_params=pltpu.CompilerParams(vmem_limit_bytes=24 * MIB),
        cost_estimate=pl.CostEstimate(
            flops=8 * part * tokens * units, bytes_accessed=2 * part * units, transcendentals=0
        ),
    )(*flat, *hiddens)


def last_step(n_tp, offsets, gate_factor, up_factor, groups, lengths, token):
    tokens, units = gate_factor.shape
    sizes = [len(g) for g in groups]
    flat = [a for g in groups for a in g]
    rows = tokens // len(offsets)
    split = 2
    half = units // split

    def body(gate_ref, up_ref, _, *refs):
        ins = refs[: len(flat)]
        gate_out, up_out, gate_buf, up_buf, sems = refs[len(flat) :]
        starts = [pl.multiple_of(s * rows, rows) for s in ring_sources(n_tp, offsets)]
        copies = []
        for h in range(split):
            cols = slice(h * half, (h + 1) * half)
            at = piece = 0
            for size, length in zip(sizes, lengths):
                for first in range(0, length, rows):
                    where = pl.ds(starts[piece], rows)
                    grad = ins[at][first : first + rows, cols].astype(F32)
                    for ref in ins[at + 1 : at + size]:
                        grad = grad + ref[first : first + rows, cols].astype(F32)
                    gate_buf[where, cols] = (grad * gate_ref[where, cols]).astype(BF16)
                    up_buf[where, cols] = (grad * up_ref[where, cols]).astype(BF16)
                    piece += 1
                at += size
            for k, (buf, out) in enumerate(((gate_buf, gate_out), (up_buf, up_out))):
                copies.append(
                    pltpu.make_async_copy(buf.at[:, cols], out.at[:, cols], sems.at[k, h])
                )
                copies[-1].start()
        for copy in copies:
            copy.wait()

    return pl.pallas_call(
        body,
        name="last_step",
        out_shape=[like(tokens, units)] * 2,
        in_specs=[VMEM] * (3 + len(flat)),
        out_specs=[HBM] * 2,
        scratch_shapes=[pltpu.VMEM((tokens, units), BF16)] * 2
        + [pltpu.SemaphoreType.DMA((2, split))],
        compiler_params=pltpu.CompilerParams(vmem_limit_bytes=16 * MIB),
        cost_estimate=pl.CostEstimate(
            flops=8 * tokens * units, bytes_accessed=16 * tokens * units, transcendentals=0
        ),
    )(gate_factor, up_factor, token, *flat)


def after(value, *others):
    return lax.optimization_barrier((value, *others))[0]


def pair_mesh(n_tp, out_grad, gate_pre, up_pre, down_weight, block_scales):
    half = n_tp // 2
    order = [2 * i for i in range(half)] + [2 * (n_tp - 1 - i) + 1 for i in range(half, n_tp)]
    up = {order[i]: order[(i + 1) % n_tp] for i in range(n_tp)}
    down = {v: k for k, v in up.items()}

    def permute(value, target):
        pairs = []
        for d in range(4):
            for t in range(n_tp):
                dd, tt = target(d, t)
                pairs.append((d * n_tp + t, dd * n_tp + tt))
        return lax.ppermute(value, BOTH, pairs)

    def flip(value, bits):
        return permute(value, lambda d, t: (d ^ bits, t))

    def send_up(value):
        return permute(value, lambda d, t: (d, up[t]))

    def send_down(value):
        return permute(value, lambda d, t: (d, down[t]))

    rows = out_grad.shape[0]
    offsets = [0]
    for k in range(1, half):
        offsets += [-k, k]
    offsets.append(half)

    own, other, send, gate_here, up_here = split_columns(out_grad, gate_pre, up_pre, 4)
    arrived = flip(send, 2)
    scales = after(block_scales, own).astype(F32)
    hidden_own, gate_factor, up_factor = hidden_quant(after(gate_here, scales), up_here)
    arrived = after(arrived, hidden_own)
    block = jnp.concatenate([own, arrived[:rows], other, arrived[rows:]], axis=0)
    weight_own = weight_rows(down_weight, after(scales, block), 4, 0)
    hidden_chip = flip(hidden_own, 2)
    hidden_core = flip(hidden_own, 1)

    got = {0: block}
    weights = None
    for k in range(1, half):
        low, high = got[1 - k], got[k - 1]
        if k == 2:
            low, high = after(low, weight_own), after(high, weight_own)
            weight_other = weight_rows(down_weight, after(scales, hidden_chip), 4, 1)
            weights = weight_own, weight_other
        if k == 3:
            low, high = after(low, weights[1]), after(high, weights[1])
        got[-k], got[k] = send_up(low), send_down(high)
    first = n_tp - 3
    hidden_far = flip(hidden_chip, 1)
    part1 = partial_hidden(
        rows,
        [[got[o]] for o in offsets[:first]],
        (after(weights[0], hidden_far, hidden_core), weights[1]),
    )
    last = [send_up(after(got[1 - half], part1[0]))]
    pieces = [[got[o]] for o in offsets[:-1]] + [last]

    sum1 = flip(part1[1], 2)
    other1 = flip(jnp.concatenate([got[o][2 * rows :] for o in offsets[:first]], axis=0), 1)
    late = [after(a, sum1) for a in last]
    other2 = flip(
        jnp.concatenate([got[o][2 * rows :] for o in offsets[first:-1]] + [late[0][2 * rows :]], axis=0), 1
    )
    part2 = partial_hidden(rows, pieces[first:-1] + [late], weights)
    sum2 = flip(part2[1], 2)
    down_grad, token = down_product(
        n_tp,
        offsets,
        pieces,
        [other1, other2],
        [hidden_own, hidden_chip, hidden_core, hidden_far],
    )
    gate_grad, up_grad = last_step(
        n_tp,
        offsets,
        gate_factor,
        up_factor,
        [[part1[0], sum1], [part2[0], sum2]],
        [first * rows, 3 * rows],
        token,
    )
    return gate_grad, up_grad, down_grad


def solution(mesh):
    n_dp, n_tp = mesh.shape["dp"], mesh.shape["tp"]

    def per_device(out_grad, gate_pre, up_pre, down_weight, block_scales):
        part = down_weight.shape[0] // n_dp
        rows = out_grad.shape[0]
        fits = (
            n_dp == 4
            and n_tp >= 8
            and n_tp % 2 == 0
            and rows % 16 == 0
            and rows * n_tp == 128
            and part % 256 == 0
            and gate_pre.shape[1] % 256 == 0
        )
        if fits:
            return pair_mesh(n_tp, out_grad, gate_pre, up_pre, down_weight, block_scales)
        return any_mesh(out_grad, gate_pre, up_pre, down_weight, block_scales)

    placed = (P(("dp", "tp"), None), P("dp", "tp"), P("dp", "tp"), P(None, "tp"), P(None, "tp"))
    return jax.shard_map(
        per_device,
        mesh=mesh,
        in_specs=placed,
        out_specs=(P("dp", "tp"), P("dp", "tp"), P("dp", "tp")),
        check_vma=False,
    )
```

```python
import jax
import jax.numpy as jnp
from jax import lax
from jax.experimental import pallas as pl
from jax.experimental.pallas import tpu as pltpu
from jax.sharding import PartitionSpec as P

BF16 = jnp.bfloat16
F32 = jnp.float32
BOTH = ("dp", "tp")
TILE = 128


def tile_quant(values, tile_axis):
    largest = jnp.max(jnp.abs(values), axis=tile_axis, keepdims=True)
    tile_scale = (largest + 1e-06) / 448.0
    payload = (values / tile_scale).astype(jnp.bfloat16)
    return (payload.astype(jnp.float32) * tile_scale).astype(jnp.bfloat16)


def fast_quant(values, tile_axis):
    largest = jnp.max(jnp.abs(values), axis=tile_axis, keepdims=True)
    tile_scale = (largest + 1e-06) / 448.0
    payload = (values * (1.0 / tile_scale)).astype(BF16)
    return (payload.astype(F32) * tile_scale).astype(BF16)


def any_mesh(out_grad, gate_pre, up_pre, down_weight, block_scales):
    width = down_weight.shape[0]
    hidden_units = down_weight.shape[1]
    weight_deq = (
        down_weight.reshape(width // 128, 128, hidden_units // 128, 128)
        * block_scales[:, None, :, None]
    ).reshape(width, hidden_units)
    grad_tokens = lax.all_gather(out_grad, "tp", axis=0, tiled=True)
    local_tokens = grad_tokens.shape[0]
    grad_full = grad_tokens.astype(jnp.float32)
    grad_rowq = tile_quant(grad_full.reshape(local_tokens, width // 128, 128), 2).reshape(
        local_tokens, width
    )
    grad_colq = tile_quant(grad_full.reshape(local_tokens // 128, 128, width), 1).reshape(
        local_tokens, width
    )
    hidden_grad = jnp.dot(grad_rowq, weight_deq, preferred_element_type=jnp.float32)
    gate_val = gate_pre.astype(jnp.float32)
    up_val = up_pre.astype(jnp.float32)
    sigma = 1.0 / (1.0 + jnp.exp(-gate_val))
    gate_grad = (hidden_grad * up_val * sigma * (1.0 + gate_val * (1.0 - sigma))).astype(
        jnp.bfloat16
    )
    up_grad = (hidden_grad * gate_val * sigma).astype(jnp.bfloat16)
    hidden_val = gate_val * sigma * up_val
    hidden_colq = tile_quant(hidden_val.reshape(local_tokens // 128, 128, hidden_units), 1).reshape(
        local_tokens, hidden_units
    )
    width_dev = width // lax.axis_size("dp")
    every_cols = lax.all_to_all(grad_colq, "dp", split_axis=1, concat_axis=0, tiled=True)
    start_sum = jnp.zeros((width_dev, hidden_units), jnp.float32)
    hidden_piece = lax.all_gather(hidden_colq, "dp", axis=0, tiled=True)
    block_count = hidden_piece.shape[0] // local_tokens

    def one_block(block_num, inner):
        hidden_block = lax.dynamic_slice_in_dim(
            hidden_piece, block_num * local_tokens, local_tokens, 0
        )
        grad_block = lax.dynamic_slice_in_dim(every_cols, block_num * local_tokens, local_tokens, 0)
        term = lax.dot_general(
            grad_block, hidden_block, (((0,), (0,)), ((), ())), preferred_element_type=jnp.float32
        )
        term = lax.optimization_barrier(term.astype(jnp.bfloat16)).astype(jnp.float32)
        return inner + term

    summed = lax.fori_loop(0, block_count, one_block, start_sum)
    return (gate_grad, up_grad, summed.astype(jnp.bfloat16))


VMEM = pl.BlockSpec(memory_space=pltpu.VMEM)
SMEM = pl.BlockSpec(memory_space=pltpu.SMEM)
HBM = pl.BlockSpec(memory_space=pltpu.HBM)
MIB = 1024 * 1024


def like(*shape, dtype=BF16):
    return jax.ShapeDtypeStruct(shape, dtype)


def ring_sources(n_tp, offsets):
    half = n_tp // 2
    me = lax.axis_index("tp")
    odd = lax.rem(me, 2)
    place = jnp.where(odd == 1, n_tp - 1 - me // 2, me // 2)
    result = []
    for offset in offsets:
        at = lax.rem(place + offset + n_tp, n_tp)
        result.append(jnp.where(at < half, 2 * at, 2 * (n_tp - 1 - at) + 1))
    return result


def split_columns(out_grad, gate_pre, up_pre, parts):
    rows, width = out_grad.shape
    part = width // parts

    def body(grad_ref, gate_ref, up_ref, own, other, send, gate_out, up_out, sems):
        me = lax.axis_index("dp")
        pairs = [
            (grad_ref.at[:, pl.ds(pl.multiple_of((me ^ flips) * part, TILE), part)], target)
            for flips, target in (
                (2, send.at[pl.ds(0, rows)]),
                (3, send.at[pl.ds(rows, rows)]),
                (0, own),
                (1, other),
            )
        ]
        pairs += [(gate_ref, gate_out), (up_ref, up_out)]
        copies = [
            pltpu.make_async_copy(source, target, sems.at[i])
            for i, (source, target) in enumerate(pairs)
        ]
        for copy in copies:
            copy.start()
        for copy in copies:
            copy.wait()

    return pl.pallas_call(
        body,
        name="split_columns",
        out_shape=[pltpu.VMEM((rows, part), BF16)] * 2
        + [pltpu.VMEM((2 * rows, part), BF16)]
        + [pltpu.VMEM(gate_pre.shape, BF16)] * 2,
        in_specs=[HBM] * 3,
        out_specs=[VMEM] * 5,
        scratch_shapes=[pltpu.SemaphoreType.DMA((6,))],
    )(out_grad, gate_pre, up_pre)


def hidden_quant(gate_pre, up_pre):
    tokens, units = gate_pre.shape

    def body(gate_ref, up_ref, hidden_ref, gate_factor, up_factor):
        for c in range(units // TILE):
            at = (slice(None), slice(c * TILE, (c + 1) * TILE))
            gate = gate_ref[at].astype(F32)
            up = up_ref[at].astype(F32)
            sigma = 1.0 / (1.0 + jnp.exp(-gate))
            hidden_ref[at] = fast_quant(gate * sigma * up, 0)
            gate_factor[at] = up * sigma * (1.0 + gate * (1.0 - sigma))
            up_factor[at] = gate * sigma

    return pl.pallas_call(
        body,
        name="hidden_quant",
        out_shape=[like(tokens, units)] + [like(tokens, units, dtype=F32)] * 2,
        in_specs=[VMEM] * 2,
        out_specs=[VMEM] * 3,
        compiler_params=pltpu.CompilerParams(vmem_limit_bytes=16 * MIB),
        cost_estimate=pl.CostEstimate(
            flops=20 * tokens * units, bytes_accessed=14 * tokens * units, transcendentals=tokens * units
        ),
    )(gate_pre, up_pre)


def weight_rows(down_weight, scales, parts, first, count):
    width, units = down_weight.shape
    part = width // parts
    chunk = TILE

    def body(scale_ref, weight_ref, out_ref, local_ref, scale_sem, sems):
        me = lax.axis_index("dp")
        get_scales = pltpu.make_async_copy(scale_ref, local_ref, scale_sem)
        get_scales.start()
        copies, blocks = [], []
        for i in range(count // chunk):
            row = first + i * chunk
            start = pl.multiple_of((me ^ (row // part)) * part + row % part, TILE)
            blocks.append((me ^ (row // part)) * (part // TILE) + row % part // TILE)
            copies.append(
                pltpu.make_async_copy(
                    weight_ref.at[pl.ds(start, chunk)],
                    out_ref.at[pl.ds(i * chunk, chunk)],
                    sems.at[i],
                )
            )
            copies[-1].start()
        get_scales.wait()
        for i in range(count // chunk):
            copies[i].wait()
            for b in range(units // TILE):
                at = (slice(i * chunk, (i + 1) * chunk), slice(b * TILE, (b + 1) * TILE))
                scale = jnp.full((TILE, TILE), local_ref[blocks[i], b], F32).astype(BF16)
                out_ref[at] = out_ref[at] * scale

    return pl.pallas_call(
        body,
        name="weight_rows",
        out_shape=like(count, units),
        in_specs=[HBM, HBM],
        out_specs=VMEM,
        scratch_shapes=[
            pltpu.SMEM(scales.shape, F32),
            pltpu.SemaphoreType.DMA,
            pltpu.SemaphoreType.DMA((count // chunk,)),
        ],
        compiler_params=pltpu.CompilerParams(vmem_limit_bytes=44 * MIB),
        cost_estimate=pl.CostEstimate(flops=count * units, bytes_accessed=4 * count * units, transcendentals=0),
    )(scales, down_weight)


def grouped(refs, sizes):
    result, at = [], 0
    for size in sizes:
        result.append(refs[at : at + size])
        at += size
    return result


def half_of(piece, h):
    return (piece[0], h * piece[0].shape[0] // 2) if len(piece) == 1 else (piece[h], 0)


def partial_hidden(rows, pieces, weights):
    sizes = [len(p) for p in pieces]
    flat = [a for p in pieces for a in p]
    part = flat[0].shape[1]
    units = weights[0].shape[1]
    each = len(pieces) * rows
    step = 512 if units % 512 == 0 else 256

    def body(*refs):
        weight_refs = refs[len(flat) : len(flat) + len(weights)]
        keep_ref, send_ref, quant_ref = refs[len(flat) + len(weights) :]
        for k, piece in enumerate(grouped(refs, sizes)):
            for h in range(2):
                ref, low = half_of(piece, h)
                for c in range(part // TILE):
                    cols = slice(c * TILE, (c + 1) * TILE)
                    deq = fast_quant(ref[low : low + 2 * rows, cols].astype(F32), 1)
                    into = slice(h * part + c * TILE, h * part + (c + 1) * TILE)
                    for s in range(2):
                        base = s * each + k * rows
                        quant_ref[base : base + rows, into] = deq[s * rows : (s + 1) * rows]
        for i in range(units // step):
            cols = slice(i * step, (i + 1) * step)
            result, at = 0.0, 0
            for ref in weight_refs:
                result += jnp.dot(
                    quant_ref[:, at : at + ref.shape[0]], ref[:, cols], preferred_element_type=F32
                )
                at += ref.shape[0]
            keep_ref[:, cols] = result[:each].astype(keep_ref.dtype)
            send_ref[:, cols] = result[each:].astype(BF16)

    return pl.pallas_call(
        body,
        name="partial_hidden",
        out_shape=[like(each, units, dtype=F32), like(each, units)],
        in_specs=[VMEM] * (len(flat) + len(weights)),
        out_specs=[VMEM] * 2,
        scratch_shapes=[pltpu.VMEM((2 * each, 2 * part), BF16)],
        compiler_params=pltpu.CompilerParams(vmem_limit_bytes=16 * MIB),
        cost_estimate=pl.CostEstimate(
            flops=8 * each * part * units, bytes_accessed=4 * part * units, transcendentals=0
        ),
    )(*flat, *weights)


def down_product(n_tp, offsets, pieces, others, hiddens):
    flat = [p[0] for p in pieces] + list(others)
    part = flat[0].shape[1]
    tokens, units = hiddens[0].shape
    rows = tokens // len(pieces)
    step, slots, split = 256, 3, 4
    steps = part // step

    def body(*refs):
        own, other = refs[: len(pieces)], refs[len(pieces) : len(flat)]
        where = [[(ref, s * rows) for ref in own] for s in range(2)]
        where += [
            [(ref, low + s * rows) for ref in other for low in range(0, ref.shape[0], 2 * rows)]
            for s in range(2)
        ]
        h_refs = refs[len(flat) : len(flat) + 4]
        out_ref, token_ref, hid_ref, quant_ref, buffer, sems = refs[len(flat) + 4 :]
        token_ref[...] = jnp.zeros(token_ref.shape, F32)
        starts = [pl.multiple_of(s * rows, rows) for s in ring_sources(n_tp, offsets)]
        for j, ref in enumerate(h_refs):
            for k, start in enumerate(starts):
                low = j * tokens + k * rows
                hid_ref[low : low + rows, :] = ref[pl.ds(start, rows), :]

        def copies(i):
            lines = step // split
            return [
                pltpu.make_async_copy(
                    buffer.at[i % slots, pl.ds(k * lines, lines)],
                    out_ref.at[pl.ds(i * step + k * lines, lines)],
                    sems.at[i % slots, k],
                )
                for k in range(split)
            ]

        for i in range(steps):
            if i >= slots:
                for copy in copies(i - slots):
                    copy.wait()
            for c in range(step // TILE):
                cols = slice(i * step + c * TILE, i * step + (c + 1) * TILE)
                for j in range(4):
                    vals = [ref[low : low + rows, cols].astype(F32) for ref, low in where[j]]
                    top = jnp.abs(vals[0])
                    for v in vals[1:]:
                        top = jnp.maximum(top, jnp.abs(v))
                    scale = (jnp.max(top, axis=0, keepdims=True) + 1e-06) / 448.0
                    inverse = 1.0 / scale
                    for k, v in enumerate(vals):
                        payload = (v * inverse).astype(BF16).astype(F32)
                        base = j * tokens + k * rows
                        quant_ref[base : base + rows, c * TILE : (c + 1) * TILE] = (
                            payload * scale
                        ).astype(BF16)
            buffer[i % slots] = lax.dot_general(
                quant_ref[...], hid_ref[...], (((0,), (0,)), ((), ())), preferred_element_type=F32
            ).astype(BF16)
            for copy in copies(i):
                copy.start()
        for i in range(max(0, steps - slots), steps):
            for copy in copies(i):
                copy.wait()

    return pl.pallas_call(
        body,
        name="down_product",
        out_shape=[like(part, units), like(8, TILE, dtype=F32)],
        in_specs=[VMEM] * (len(flat) + 4),
        out_specs=[HBM, VMEM],
        scratch_shapes=[
            pltpu.VMEM((4 * tokens, units), BF16),
            pltpu.VMEM((4 * tokens, step), BF16),
            pltpu.VMEM((slots, step, units), BF16),
            pltpu.SemaphoreType.DMA((slots, split)),
        ],
        compiler_params=pltpu.CompilerParams(vmem_limit_bytes=24 * MIB),
        cost_estimate=pl.CostEstimate(
            flops=8 * part * tokens * units, bytes_accessed=2 * part * units, transcendentals=0
        ),
    )(*flat, *hiddens)


def last_step(n_tp, offsets, gate_factor, up_factor, groups, lengths, token):
    tokens, units = gate_factor.shape
    sizes = [len(g) for g in groups]
    flat = [a for g in groups for a in g]
    rows = tokens // len(offsets)
    split = 2
    half = units // split

    def body(gate_ref, up_ref, _, *refs):
        ins = refs[: len(flat)]
        gate_out, up_out, gate_buf, up_buf, sems = refs[len(flat) :]
        starts = [pl.multiple_of(s * rows, rows) for s in ring_sources(n_tp, offsets)]
        copies = []
        for h in range(split):
            cols = slice(h * half, (h + 1) * half)
            at = piece = 0
            for size, length in zip(sizes, lengths):
                for first in range(0, length, rows):
                    where = pl.ds(starts[piece], rows)
                    grad = ins[at][first : first + rows, cols].astype(F32)
                    for ref in ins[at + 1 : at + size]:
                        grad = grad + ref[first : first + rows, cols].astype(F32)
                    gate_buf[where, cols] = (grad * gate_ref[where, cols]).astype(BF16)
                    up_buf[where, cols] = (grad * up_ref[where, cols]).astype(BF16)
                    piece += 1
                at += size
            for k, (buf, out) in enumerate(((gate_buf, gate_out), (up_buf, up_out))):
                copies.append(
                    pltpu.make_async_copy(buf.at[:, cols], out.at[:, cols], sems.at[k, h])
                )
                copies[-1].start()
        for copy in copies:
            copy.wait()

    return pl.pallas_call(
        body,
        name="last_step",
        out_shape=[like(tokens, units)] * 2,
        in_specs=[VMEM] * (3 + len(flat)),
        out_specs=[HBM] * 2,
        scratch_shapes=[pltpu.VMEM((tokens, units), BF16)] * 2
        + [pltpu.SemaphoreType.DMA((2, split))],
        compiler_params=pltpu.CompilerParams(vmem_limit_bytes=16 * MIB),
        cost_estimate=pl.CostEstimate(
            flops=8 * tokens * units, bytes_accessed=16 * tokens * units, transcendentals=0
        ),
    )(gate_factor, up_factor, token, *flat)


def after(value, *others):
    return lax.optimization_barrier((value, *others))[0]


def pair_mesh(n_tp, out_grad, gate_pre, up_pre, down_weight, block_scales):
    half = n_tp // 2
    order = [2 * i for i in range(half)] + [2 * (n_tp - 1 - i) + 1 for i in range(half, n_tp)]
    up = {order[i]: order[(i + 1) % n_tp] for i in range(n_tp)}
    down = {v: k for k, v in up.items()}

    def permute(value, target):
        pairs = []
        for d in range(4):
            for t in range(n_tp):
                dd, tt = target(d, t)
                pairs.append((d * n_tp + t, dd * n_tp + tt))
        return lax.ppermute(value, BOTH, pairs)

    def flip(value, bits):
        return permute(value, lambda d, t: (d ^ bits, t))

    def send_up(value):
        return permute(value, lambda d, t: (d, up[t]))

    def send_down(value):
        return permute(value, lambda d, t: (d, down[t]))

    rows = out_grad.shape[0]
    offsets = [0]
    for k in range(1, half):
        offsets += [-k, k]
    offsets.append(half)

    own, other, send, gate_here, up_here = split_columns(out_grad, gate_pre, up_pre, 4)
    arrived = flip(send, 2)
    scales = after(block_scales, own).astype(F32)
    hidden_own, gate_factor, up_factor = hidden_quant(after(gate_here, scales), up_here)
    part = own.shape[1]
    tiles = 2 * part // 256
    cuts = [0, 256 * (tiles * 3 // 14), 256 * (tiles * 10 // 14), 2 * part]

    def weight_cut(i, *others):
        return weight_rows(down_weight, after(scales, *others), 4, cuts[i], cuts[i + 1] - cuts[i])

    weight0 = weight_cut(0, hidden_own)
    arrived = after(arrived, weight0)
    block = jnp.concatenate([own, arrived[:rows], other, arrived[rows:]], axis=0)
    weight1 = weight_cut(1, block)
    hidden_chip = flip(hidden_own, 2)

    got = {0: block}
    weights = None
    for k in range(1, half):
        low, high = got[1 - k], got[k - 1]
        if k == 2:
            low, high = after(low, weight1), after(high, weight1)
            weight2 = weight_cut(2, hidden_chip)
            weights = weight0, weight1, weight2
        if k == 3:
            low, high = after(low, weight2), after(high, weight2)
        got[-k], got[k] = send_up(low), send_down(high)
    first = n_tp - 4
    part1 = partial_hidden(
        rows,
        [[got[o]] for o in offsets[:first]],
        weights,
    )
    last = [send_up(after(got[1 - half], part1[0]))]
    pieces = [[got[o]] for o in offsets[:-1]] + [last]

    sum1 = flip(part1[1], 2)
    hidden_core = flip(after(hidden_own, sum1), 1)
    hidden_far = flip(after(hidden_chip, sum1), 1)
    other1 = flip(jnp.concatenate([got[o][2 * rows :] for o in offsets[:first]], axis=0), 1)
    late = [after(a, sum1) for a in last]
    other2 = flip(
        jnp.concatenate([got[o][2 * rows :] for o in offsets[first:-1]] + [late[0][2 * rows :]], axis=0), 1
    )
    part2 = partial_hidden(rows, pieces[first:-1] + [late], weights)
    sum2 = flip(part2[1], 2)
    down_grad, token = down_product(
        n_tp,
        offsets,
        pieces,
        [other1, other2],
        [hidden_own, hidden_chip, hidden_core, hidden_far],
    )
    gate_grad, up_grad = last_step(
        n_tp,
        offsets,
        gate_factor,
        up_factor,
        [[part1[0], sum1], [part2[0], sum2]],
        [first * rows, (n_tp - first) * rows],
        token,
    )
    return gate_grad, up_grad, down_grad


def solution(mesh):
    n_dp, n_tp = mesh.shape["dp"], mesh.shape["tp"]

    def per_device(out_grad, gate_pre, up_pre, down_weight, block_scales):
        part = down_weight.shape[0] // n_dp
        rows = out_grad.shape[0]
        fits = (
            n_dp == 4
            and n_tp >= 8
            and n_tp % 2 == 0
            and rows % 16 == 0
            and rows * n_tp == 128
            and part % 256 == 0
            and part >= 1024
            and gate_pre.shape[1] % 256 == 0
        )
        if fits:
            return pair_mesh(n_tp, out_grad, gate_pre, up_pre, down_weight, block_scales)
        return any_mesh(out_grad, gate_pre, up_pre, down_weight, block_scales)

    placed = (P(("dp", "tp"), None), P("dp", "tp"), P("dp", "tp"), P(None, "tp"), P(None, "tp"))
    return jax.shard_map(
        per_device,
        mesh=mesh,
        in_specs=placed,
        out_specs=(P("dp", "tp"), P("dp", "tp"), P("dp", "tp")),
        check_vma=False,
    )
```

```python
import jax
import jax.numpy as jnp
from jax import lax
from jax.experimental import pallas as pl
from jax.experimental.pallas import tpu as pltpu
from jax.sharding import PartitionSpec as P

BF16 = jnp.bfloat16
F32 = jnp.float32
BOTH = ("dp", "tp")
TILE = 128


def tile_quant(values, tile_axis):
    largest = jnp.max(jnp.abs(values), axis=tile_axis, keepdims=True)
    tile_scale = (largest + 1e-06) / 448.0
    payload = (values / tile_scale).astype(jnp.bfloat16)
    return (payload.astype(jnp.float32) * tile_scale).astype(jnp.bfloat16)


def fast_quant(values, tile_axis):
    largest = jnp.max(jnp.abs(values), axis=tile_axis, keepdims=True)
    tile_scale = (largest + 1e-06) / 448.0
    payload = (values * (1.0 / tile_scale)).astype(BF16)
    return (payload.astype(F32) * tile_scale).astype(BF16)


def any_mesh(out_grad, gate_pre, up_pre, down_weight, block_scales):
    width = down_weight.shape[0]
    hidden_units = down_weight.shape[1]
    weight_deq = (
        down_weight.reshape(width // 128, 128, hidden_units // 128, 128)
        * block_scales[:, None, :, None]
    ).reshape(width, hidden_units)
    grad_tokens = lax.all_gather(out_grad, "tp", axis=0, tiled=True)
    local_tokens = grad_tokens.shape[0]
    grad_full = grad_tokens.astype(jnp.float32)
    grad_rowq = tile_quant(grad_full.reshape(local_tokens, width // 128, 128), 2).reshape(
        local_tokens, width
    )
    grad_colq = tile_quant(grad_full.reshape(local_tokens // 128, 128, width), 1).reshape(
        local_tokens, width
    )
    hidden_grad = jnp.dot(grad_rowq, weight_deq, preferred_element_type=jnp.float32)
    gate_val = gate_pre.astype(jnp.float32)
    up_val = up_pre.astype(jnp.float32)
    sigma = 1.0 / (1.0 + jnp.exp(-gate_val))
    gate_grad = (hidden_grad * up_val * sigma * (1.0 + gate_val * (1.0 - sigma))).astype(
        jnp.bfloat16
    )
    up_grad = (hidden_grad * gate_val * sigma).astype(jnp.bfloat16)
    hidden_val = gate_val * sigma * up_val
    hidden_colq = tile_quant(hidden_val.reshape(local_tokens // 128, 128, hidden_units), 1).reshape(
        local_tokens, hidden_units
    )
    width_dev = width // lax.axis_size("dp")
    every_cols = lax.all_to_all(grad_colq, "dp", split_axis=1, concat_axis=0, tiled=True)
    start_sum = jnp.zeros((width_dev, hidden_units), jnp.float32)
    hidden_piece = lax.all_gather(hidden_colq, "dp", axis=0, tiled=True)
    block_count = hidden_piece.shape[0] // local_tokens

    def one_block(block_num, inner):
        hidden_block = lax.dynamic_slice_in_dim(
            hidden_piece, block_num * local_tokens, local_tokens, 0
        )
        grad_block = lax.dynamic_slice_in_dim(every_cols, block_num * local_tokens, local_tokens, 0)
        term = lax.dot_general(
            grad_block, hidden_block, (((0,), (0,)), ((), ())), preferred_element_type=jnp.float32
        )
        term = lax.optimization_barrier(term.astype(jnp.bfloat16)).astype(jnp.float32)
        return inner + term

    summed = lax.fori_loop(0, block_count, one_block, start_sum)
    return (gate_grad, up_grad, summed.astype(jnp.bfloat16))


VMEM = pl.BlockSpec(memory_space=pltpu.VMEM)
SMEM = pl.BlockSpec(memory_space=pltpu.SMEM)
HBM = pl.BlockSpec(memory_space=pltpu.HBM)
MIB = 1024 * 1024


def like(*shape, dtype=BF16):
    return jax.ShapeDtypeStruct(shape, dtype)


def ring_sources(n_tp, offsets):
    half = n_tp // 2
    me = lax.axis_index("tp")
    odd = lax.rem(me, 2)
    place = jnp.where(odd == 1, n_tp - 1 - me // 2, me // 2)
    result = []
    for offset in offsets:
        at = lax.rem(place + offset + n_tp, n_tp)
        result.append(jnp.where(at < half, 2 * at, 2 * (n_tp - 1 - at) + 1))
    return result


def split_columns(out_grad, gate_pre, up_pre, parts):
    rows, width = out_grad.shape
    part = width // parts

    def body(grad_ref, gate_ref, up_ref, own, other, send, gate_out, up_out, sems):
        me = lax.axis_index("dp")
        pairs = [
            (grad_ref.at[:, pl.ds(pl.multiple_of((me ^ flips) * part, TILE), part)], target)
            for flips, target in (
                (2, send.at[pl.ds(0, rows)]),
                (3, send.at[pl.ds(rows, rows)]),
                (0, own),
                (1, other),
            )
        ]
        pairs += [(gate_ref, gate_out), (up_ref, up_out)]
        copies = [
            pltpu.make_async_copy(source, target, sems.at[i])
            for i, (source, target) in enumerate(pairs)
        ]
        for copy in copies:
            copy.start()
        for copy in copies:
            copy.wait()

    return pl.pallas_call(
        body,
        name="split_columns",
        out_shape=[pltpu.VMEM((rows, part), BF16)] * 2
        + [pltpu.VMEM((2 * rows, part), BF16)]
        + [pltpu.VMEM(gate_pre.shape, BF16)] * 2,
        in_specs=[HBM] * 3,
        out_specs=[VMEM] * 5,
        scratch_shapes=[pltpu.SemaphoreType.DMA((6,))],
    )(out_grad, gate_pre, up_pre)


def hidden_quant(gate_pre, up_pre):
    tokens, units = gate_pre.shape

    def body(gate_ref, up_ref, hidden_ref, gate_factor, up_factor):
        for c in range(units // TILE):
            at = (slice(None), slice(c * TILE, (c + 1) * TILE))
            gate = gate_ref[at].astype(F32)
            up = up_ref[at].astype(F32)
            sigma = 1.0 / (1.0 + jnp.exp(-gate))
            hidden_ref[at] = fast_quant(gate * sigma * up, 0)
            gate_factor[at] = up * sigma * (1.0 + gate * (1.0 - sigma))
            up_factor[at] = gate * sigma

    return pl.pallas_call(
        body,
        name="hidden_quant",
        out_shape=[like(tokens, units)] + [like(tokens, units, dtype=F32)] * 2,
        in_specs=[VMEM] * 2,
        out_specs=[VMEM] * 3,
        compiler_params=pltpu.CompilerParams(vmem_limit_bytes=16 * MIB),
        cost_estimate=pl.CostEstimate(
            flops=20 * tokens * units, bytes_accessed=14 * tokens * units, transcendentals=tokens * units
        ),
    )(gate_pre, up_pre)


def weight_rows(down_weight, scales, parts, first, count):
    width, units = down_weight.shape
    part = width // parts
    chunk = TILE

    def body(scale_ref, weight_ref, out_ref, local_ref, scale_sem, sems):
        me = lax.axis_index("dp")
        get_scales = pltpu.make_async_copy(scale_ref, local_ref, scale_sem)
        get_scales.start()
        copies, blocks = [], []
        for i in range(count // chunk):
            row = first + i * chunk
            start = pl.multiple_of((me ^ (row // part)) * part + row % part, TILE)
            blocks.append((me ^ (row // part)) * (part // TILE) + row % part // TILE)
            copies.append(
                pltpu.make_async_copy(
                    weight_ref.at[pl.ds(start, chunk)],
                    out_ref.at[pl.ds(i * chunk, chunk)],
                    sems.at[i],
                )
            )
            copies[-1].start()
        get_scales.wait()
        for i in range(count // chunk):
            copies[i].wait()
            for b in range(units // TILE):
                at = (slice(i * chunk, (i + 1) * chunk), slice(b * TILE, (b + 1) * TILE))
                scale = jnp.full((TILE, TILE), local_ref[blocks[i], b], F32).astype(BF16)
                out_ref[at] = out_ref[at] * scale

    return pl.pallas_call(
        body,
        name="weight_rows",
        out_shape=like(count, units),
        in_specs=[HBM, HBM],
        out_specs=VMEM,
        scratch_shapes=[
            pltpu.SMEM(scales.shape, F32),
            pltpu.SemaphoreType.DMA,
            pltpu.SemaphoreType.DMA((count // chunk,)),
        ],
        compiler_params=pltpu.CompilerParams(vmem_limit_bytes=44 * MIB),
        cost_estimate=pl.CostEstimate(flops=count * units, bytes_accessed=4 * count * units, transcendentals=0),
    )(scales, down_weight)


def grouped(refs, sizes):
    result, at = [], 0
    for size in sizes:
        result.append(refs[at : at + size])
        at += size
    return result


def half_of(piece, h):
    return (piece[0], h * piece[0].shape[0] // 2) if len(piece) == 1 else (piece[h], 0)


def partial_hidden(rows, pieces, weights):
    sizes = [len(p) for p in pieces]
    flat = [a for p in pieces for a in p]
    part = flat[0].shape[1]
    units = weights[0].shape[1]
    each = len(pieces) * rows
    step = 512 if units % 512 == 0 else 256

    def body(*refs):
        weight_refs = refs[len(flat) : len(flat) + len(weights)]
        keep_ref, send_ref, quant_ref = refs[len(flat) + len(weights) :]
        for k, piece in enumerate(grouped(refs, sizes)):
            for h in range(2):
                ref, low = half_of(piece, h)
                for c in range(part // TILE):
                    cols = slice(c * TILE, (c + 1) * TILE)
                    deq = fast_quant(ref[low : low + 2 * rows, cols].astype(F32), 1)
                    into = slice(h * part + c * TILE, h * part + (c + 1) * TILE)
                    for s in range(2):
                        base = s * each + k * rows
                        quant_ref[base : base + rows, into] = deq[s * rows : (s + 1) * rows]
        for i in range(units // step):
            cols = slice(i * step, (i + 1) * step)
            result, at = 0.0, 0
            for ref in weight_refs:
                result += jnp.dot(
                    quant_ref[:, at : at + ref.shape[0]], ref[:, cols], preferred_element_type=F32
                )
                at += ref.shape[0]
            keep_ref[:, cols] = result[:each].astype(keep_ref.dtype)
            send_ref[:, cols] = result[each:].astype(BF16)

    return pl.pallas_call(
        body,
        name="partial_hidden",
        out_shape=[like(each, units, dtype=F32), like(each, units)],
        in_specs=[VMEM] * (len(flat) + len(weights)),
        out_specs=[VMEM] * 2,
        scratch_shapes=[pltpu.VMEM((2 * each, 2 * part), BF16)],
        compiler_params=pltpu.CompilerParams(vmem_limit_bytes=16 * MIB),
        cost_estimate=pl.CostEstimate(
            flops=8 * each * part * units, bytes_accessed=4 * part * units, transcendentals=0
        ),
    )(*flat, *weights)


def down_product(n_tp, offsets, pieces, others, hiddens):
    flat = [p[0] for p in pieces] + list(others)
    part = flat[0].shape[1]
    tokens, units = hiddens[0].shape
    rows = tokens // len(pieces)
    slots, split = 3, 4
    step = 512 if part > 512 else 128
    steps, at = [], 0
    while at < part:
        size = min(step, part - at)
        cut = at + size == part and size > TILE
        steps += [(at, size - TILE), (at + size - TILE, TILE)] if cut else [(at, size)]
        at += size
    widest = max(size for _, size in steps)
    third = units // 3 if units % (3 * TILE) == 0 else units

    def body(*refs):
        own, other = refs[: len(pieces)], refs[len(pieces) : len(flat)]
        where = [[(ref, s * rows) for ref in own] for s in range(2)]
        where += [
            [(ref, low + s * rows) for ref in other for low in range(0, ref.shape[0], 2 * rows)]
            for s in range(2)
        ]
        h_refs = refs[len(flat) : len(flat) + 4]
        out_ref, token_ref, hid_ref, quant_ref, buffer, sems = refs[len(flat) + 4 :]
        token_ref[...] = jnp.zeros(token_ref.shape, F32)
        starts = [pl.multiple_of(s * rows, rows) for s in ring_sources(n_tp, offsets)]
        for j, ref in enumerate(h_refs):
            for k, start in enumerate(starts):
                low = j * tokens + k * rows
                hid_ref[low : low + rows, :] = ref[pl.ds(start, rows), :]

        def copies(i):
            at, size = steps[i]
            lines = size // split
            return [
                pltpu.make_async_copy(
                    buffer.at[i % slots, pl.ds(k * lines, lines)],
                    out_ref.at[pl.ds(at + k * lines, lines)],
                    sems.at[i % slots, k],
                )
                for k in range(split)
            ]

        for i, (at, size) in enumerate(steps):
            if i >= slots:
                for copy in copies(i - slots):
                    copy.wait()
            for c in range(size // TILE):
                cols = slice(at + c * TILE, at + (c + 1) * TILE)
                for j in range(4):
                    vals = [ref[low : low + rows, cols].astype(F32) for ref, low in where[j]]
                    top = jnp.abs(vals[0])
                    for v in vals[1:]:
                        top = jnp.maximum(top, jnp.abs(v))
                    scale = (jnp.max(top, axis=0, keepdims=True) + 1e-06) / 448.0
                    inverse = 1.0 / scale
                    for k, v in enumerate(vals):
                        payload = (v * inverse).astype(BF16).astype(F32)
                        base = j * tokens + k * rows
                        quant_ref[base : base + rows, c * TILE : (c + 1) * TILE] = (
                            payload * scale
                        ).astype(BF16)
            for low in range(0, units, third):
                hidden = hid_ref[:, low : low + third]
                buffer[i % slots, :size, low : low + third] = lax.dot_general(
                    quant_ref[:, :size], hidden, (((0,), (0,)), ((), ())), preferred_element_type=F32
                ).astype(BF16)
            for copy in copies(i):
                copy.start()
        for i in range(max(0, len(steps) - slots), len(steps)):
            for copy in copies(i):
                copy.wait()

    return pl.pallas_call(
        body,
        name="down_product",
        out_shape=[like(part, units), like(8, TILE, dtype=F32)],
        in_specs=[VMEM] * (len(flat) + 4),
        out_specs=[HBM, VMEM],
        scratch_shapes=[
            pltpu.VMEM((4 * tokens, units), BF16),
            pltpu.VMEM((4 * tokens, widest), BF16),
            pltpu.VMEM((slots, widest, units), BF16),
            pltpu.SemaphoreType.DMA((slots, split)),
        ],
        compiler_params=pltpu.CompilerParams(vmem_limit_bytes=24 * MIB),
        cost_estimate=pl.CostEstimate(
            flops=8 * part * tokens * units, bytes_accessed=2 * part * units, transcendentals=0
        ),
    )(*flat, *hiddens)


def last_step(n_tp, offsets, gate_factor, up_factor, groups, lengths, token):
    tokens, units = gate_factor.shape
    sizes = [len(g) for g in groups]
    flat = [a for g in groups for a in g]
    rows = tokens // len(offsets)
    split = 2
    half = units // split

    def body(gate_ref, up_ref, _, *refs):
        ins = refs[: len(flat)]
        gate_out, up_out, gate_buf, up_buf, sems = refs[len(flat) :]
        starts = [pl.multiple_of(s * rows, rows) for s in ring_sources(n_tp, offsets)]
        copies = []
        for h in range(split):
            cols = slice(h * half, (h + 1) * half)
            at = piece = 0
            for size, length in zip(sizes, lengths):
                for first in range(0, length, rows):
                    where = pl.ds(starts[piece], rows)
                    grad = ins[at][first : first + rows, cols].astype(F32)
                    for ref in ins[at + 1 : at + size]:
                        grad = grad + ref[first : first + rows, cols].astype(F32)
                    gate_buf[where, cols] = (grad * gate_ref[where, cols]).astype(BF16)
                    up_buf[where, cols] = (grad * up_ref[where, cols]).astype(BF16)
                    piece += 1
                at += size
            for k, (buf, out) in enumerate(((gate_buf, gate_out), (up_buf, up_out))):
                copies.append(
                    pltpu.make_async_copy(buf.at[:, cols], out.at[:, cols], sems.at[k, h])
                )
                copies[-1].start()
        for copy in copies:
            copy.wait()

    return pl.pallas_call(
        body,
        name="last_step",
        out_shape=[like(tokens, units)] * 2,
        in_specs=[VMEM] * (3 + len(flat)),
        out_specs=[HBM] * 2,
        scratch_shapes=[pltpu.VMEM((tokens, units), BF16)] * 2
        + [pltpu.SemaphoreType.DMA((2, split))],
        compiler_params=pltpu.CompilerParams(vmem_limit_bytes=16 * MIB),
        cost_estimate=pl.CostEstimate(
            flops=8 * tokens * units, bytes_accessed=16 * tokens * units, transcendentals=0
        ),
    )(gate_factor, up_factor, token, *flat)


def after(value, *others):
    return lax.optimization_barrier((value, *others))[0]


def pair_mesh(n_tp, out_grad, gate_pre, up_pre, down_weight, block_scales):
    half = n_tp // 2
    order = [2 * i for i in range(half)] + [2 * (n_tp - 1 - i) + 1 for i in range(half, n_tp)]
    up = {order[i]: order[(i + 1) % n_tp] for i in range(n_tp)}
    down = {v: k for k, v in up.items()}

    def permute(value, target):
        pairs = []
        for d in range(4):
            for t in range(n_tp):
                dd, tt = target(d, t)
                pairs.append((d * n_tp + t, dd * n_tp + tt))
        return lax.ppermute(value, BOTH, pairs)

    def flip(value, bits):
        return permute(value, lambda d, t: (d ^ bits, t))

    def send_up(value):
        return permute(value, lambda d, t: (d, up[t]))

    def send_down(value):
        return permute(value, lambda d, t: (d, down[t]))

    rows = out_grad.shape[0]
    offsets = [0]
    for k in range(1, half):
        offsets += [k, -k]
    offsets.append(half)

    own, other, send, gate_here, up_here = split_columns(out_grad, gate_pre, up_pre, 4)
    arrived = flip(send, 2)
    scales = after(block_scales, own).astype(F32)
    hidden_own, gate_factor, up_factor = hidden_quant(after(gate_here, scales), up_here)
    part = own.shape[1]
    tiles = 2 * part // 256
    cuts = [0, 256 * (tiles * 3 // 14), 256 * (tiles * 10 // 14), 2 * part]

    def weight_cut(i, *others):
        return weight_rows(down_weight, after(scales, *others), 4, cuts[i], cuts[i + 1] - cuts[i])

    weight0 = weight_cut(0, hidden_own)
    arrived = after(arrived, weight0)
    block = jnp.concatenate([own, arrived[:rows], other, arrived[rows:]], axis=0)
    weight1 = weight_cut(1, block)
    hidden_chip = flip(hidden_own, 2)
    hidden_core = flip(hidden_own, 1)

    got = {0: block}
    for k in range(1, half):
        low, high = got[1 - k], got[k - 1]
        if k == 2:
            low, high = after(low, weight1), after(high, weight1)
            weight2 = weight_cut(2, hidden_core)
            weights = weight0, weight1, weight2
            part1 = partial_hidden(rows, [[got[o]] for o in offsets[:3]], weights)
        if k == 3:
            low, high = after(low, part1[0]), after(high, part1[0])
        got[-k], got[k] = send_up(low), send_down(high)
    first = n_tp - 3
    part2 = partial_hidden(rows, [[got[o]] for o in offsets[3:first]], weights)
    hidden_far = flip(after(hidden_chip, got[1 - half], got[half - 1]), 1)
    last = [send_up(after(got[1 - half], part2[0]))]
    pieces = [[got[o]] for o in offsets[:-1]] + [last]

    sum1 = flip(part1[1], 2)
    sum2 = flip(part2[1], 2)
    other1 = flip(jnp.concatenate([got[o][2 * rows :] for o in offsets[:first]], axis=0), 1)
    late = [after(a, sum1, sum2) for a in last]
    tail = after(late[0], hidden_far)
    other2 = flip(
        jnp.concatenate([got[o][2 * rows :] for o in offsets[first:-1]] + [tail[2 * rows :]], axis=0), 1
    )
    part3 = partial_hidden(rows, pieces[first:-1] + [late], weights)
    sum3 = flip(part3[1], 2)
    down_grad, token = down_product(
        n_tp,
        offsets,
        pieces,
        [other1, other2],
        [hidden_own, hidden_chip, hidden_core, hidden_far],
    )
    gate_grad, up_grad = last_step(
        n_tp,
        offsets,
        gate_factor,
        up_factor,
        [[part1[0], sum1], [part2[0], sum2], [part3[0], sum3]],
        [3 * rows, (first - 3) * rows, 3 * rows],
        token,
    )
    return gate_grad, up_grad, down_grad


def solution(mesh):
    n_dp, n_tp = mesh.shape["dp"], mesh.shape["tp"]

    def per_device(out_grad, gate_pre, up_pre, down_weight, block_scales):
        part = down_weight.shape[0] // n_dp
        rows = out_grad.shape[0]
        fits = (
            n_dp == 4
            and n_tp >= 8
            and n_tp % 2 == 0
            and rows % 16 == 0
            and rows * n_tp == 128
            and part % 256 == 0
            and part >= 1024
            and gate_pre.shape[1] % 256 == 0
        )
        if fits:
            return pair_mesh(n_tp, out_grad, gate_pre, up_pre, down_weight, block_scales)
        return any_mesh(out_grad, gate_pre, up_pre, down_weight, block_scales)

    placed = (P(("dp", "tp"), None), P("dp", "tp"), P("dp", "tp"), P(None, "tp"), P(None, "tp"))
    return jax.shard_map(
        per_device,
        mesh=mesh,
        in_specs=placed,
        out_specs=(P("dp", "tp"), P("dp", "tp"), P("dp", "tp")),
        check_vma=False,
    )
```

```python
import jax
import jax.numpy as jnp
from jax import lax
from jax.experimental import pallas as pl
from jax.experimental.pallas import tpu as pltpu
from jax.sharding import PartitionSpec as P

BF16 = jnp.bfloat16
F32 = jnp.float32
BOTH = ("dp", "tp")
TILE = 128


def tile_quant(values, tile_axis):
    largest = jnp.max(jnp.abs(values), axis=tile_axis, keepdims=True)
    tile_scale = (largest + 1e-06) / 448.0
    payload = (values / tile_scale).astype(jnp.bfloat16)
    return (payload.astype(jnp.float32) * tile_scale).astype(jnp.bfloat16)


def fast_quant(values, tile_axis):
    largest = jnp.max(jnp.abs(values), axis=tile_axis, keepdims=True)
    tile_scale = (largest + 1e-06) / 448.0
    payload = (values * (1.0 / tile_scale)).astype(BF16)
    return (payload.astype(F32) * tile_scale).astype(BF16)


def any_mesh(out_grad, gate_pre, up_pre, down_weight, block_scales):
    width = down_weight.shape[0]
    hidden_units = down_weight.shape[1]
    weight_deq = (
        down_weight.reshape(width // 128, 128, hidden_units // 128, 128)
        * block_scales[:, None, :, None]
    ).reshape(width, hidden_units)
    grad_tokens = lax.all_gather(out_grad, "tp", axis=0, tiled=True)
    local_tokens = grad_tokens.shape[0]
    grad_full = grad_tokens.astype(jnp.float32)
    grad_rowq = tile_quant(grad_full.reshape(local_tokens, width // 128, 128), 2).reshape(
        local_tokens, width
    )
    grad_colq = tile_quant(grad_full.reshape(local_tokens // 128, 128, width), 1).reshape(
        local_tokens, width
    )
    hidden_grad = jnp.dot(grad_rowq, weight_deq, preferred_element_type=jnp.float32)
    gate_val = gate_pre.astype(jnp.float32)
    up_val = up_pre.astype(jnp.float32)
    sigma = 1.0 / (1.0 + jnp.exp(-gate_val))
    gate_grad = (hidden_grad * up_val * sigma * (1.0 + gate_val * (1.0 - sigma))).astype(
        jnp.bfloat16
    )
    up_grad = (hidden_grad * gate_val * sigma).astype(jnp.bfloat16)
    hidden_val = gate_val * sigma * up_val
    hidden_colq = tile_quant(hidden_val.reshape(local_tokens // 128, 128, hidden_units), 1).reshape(
        local_tokens, hidden_units
    )
    width_dev = width // lax.axis_size("dp")
    every_cols = lax.all_to_all(grad_colq, "dp", split_axis=1, concat_axis=0, tiled=True)
    start_sum = jnp.zeros((width_dev, hidden_units), jnp.float32)
    hidden_piece = lax.all_gather(hidden_colq, "dp", axis=0, tiled=True)
    block_count = hidden_piece.shape[0] // local_tokens

    def one_block(block_num, inner):
        hidden_block = lax.dynamic_slice_in_dim(
            hidden_piece, block_num * local_tokens, local_tokens, 0
        )
        grad_block = lax.dynamic_slice_in_dim(every_cols, block_num * local_tokens, local_tokens, 0)
        term = lax.dot_general(
            grad_block, hidden_block, (((0,), (0,)), ((), ())), preferred_element_type=jnp.float32
        )
        term = lax.optimization_barrier(term.astype(jnp.bfloat16)).astype(jnp.float32)
        return inner + term

    summed = lax.fori_loop(0, block_count, one_block, start_sum)
    return (gate_grad, up_grad, summed.astype(jnp.bfloat16))


VMEM = pl.BlockSpec(memory_space=pltpu.VMEM)
SMEM = pl.BlockSpec(memory_space=pltpu.SMEM)
HBM = pl.BlockSpec(memory_space=pltpu.HBM)
MIB = 1024 * 1024


def like(*shape, dtype=BF16):
    return jax.ShapeDtypeStruct(shape, dtype)


def ring_sources(n_tp, offsets):
    half = n_tp // 2
    me = lax.axis_index("tp")
    odd = lax.rem(me, 2)
    place = jnp.where(odd == 1, n_tp - 1 - me // 2, me // 2)
    result = []
    for offset in offsets:
        at = lax.rem(place + offset + n_tp, n_tp)
        result.append(jnp.where(at < half, 2 * at, 2 * (n_tp - 1 - at) + 1))
    return result


def split_columns(out_grad, gate_pre, up_pre, parts):
    rows, width = out_grad.shape
    part = width // parts

    def body(grad_ref, gate_ref, up_ref, own, other, send, gate_out, up_out, sems):
        me = lax.axis_index("dp")
        pairs = [
            (grad_ref.at[:, pl.ds(pl.multiple_of((me ^ flips) * part, TILE), part)], target)
            for flips, target in (
                (2, send.at[pl.ds(0, rows)]),
                (3, send.at[pl.ds(rows, rows)]),
                (0, own),
                (1, other),
            )
        ]
        pairs += [(gate_ref, gate_out), (up_ref, up_out)]
        copies = [
            pltpu.make_async_copy(source, target, sems.at[i])
            for i, (source, target) in enumerate(pairs)
        ]
        for copy in copies:
            copy.start()
        for copy in copies:
            copy.wait()

    return pl.pallas_call(
        body,
        name="split_columns",
        out_shape=[pltpu.VMEM((rows, part), BF16)] * 2
        + [pltpu.VMEM((2 * rows, part), BF16)]
        + [pltpu.VMEM(gate_pre.shape, BF16)] * 2,
        in_specs=[HBM] * 3,
        out_specs=[VMEM] * 5,
        scratch_shapes=[pltpu.SemaphoreType.DMA((6,))],
    )(out_grad, gate_pre, up_pre)


def hidden_quant(gate_pre, up_pre):
    tokens, units = gate_pre.shape

    def body(gate_ref, up_ref, hidden_ref, gate_factor, up_factor):
        for c in range(units // TILE):
            at = (slice(None), slice(c * TILE, (c + 1) * TILE))
            gate = gate_ref[at].astype(F32)
            up = up_ref[at].astype(F32)
            sigma = 1.0 / (1.0 + jnp.exp(-gate))
            hidden_ref[at] = fast_quant(gate * sigma * up, 0)
            gate_factor[at] = up * sigma * (1.0 + gate * (1.0 - sigma))
            up_factor[at] = gate * sigma

    return pl.pallas_call(
        body,
        name="hidden_quant",
        out_shape=[like(tokens, units)] + [like(tokens, units, dtype=F32)] * 2,
        in_specs=[VMEM] * 2,
        out_specs=[VMEM] * 3,
        compiler_params=pltpu.CompilerParams(vmem_limit_bytes=16 * MIB),
        cost_estimate=pl.CostEstimate(
            flops=20 * tokens * units, bytes_accessed=14 * tokens * units, transcendentals=tokens * units
        ),
    )(gate_pre, up_pre)


def weight_rows(down_weight, scales, parts, first, count):
    width, units = down_weight.shape
    part = width // parts
    chunk = TILE

    def body(scale_ref, weight_ref, out_ref, local_ref, scale_sem, sems):
        me = lax.axis_index("dp")
        get_scales = pltpu.make_async_copy(scale_ref, local_ref, scale_sem)
        get_scales.start()
        copies, blocks = [], []
        for i in range(count // chunk):
            row = first + i * chunk
            start = pl.multiple_of((me ^ (row // part)) * part + row % part, TILE)
            blocks.append((me ^ (row // part)) * (part // TILE) + row % part // TILE)
            copies.append(
                pltpu.make_async_copy(
                    weight_ref.at[pl.ds(start, chunk)],
                    out_ref.at[pl.ds(i * chunk, chunk)],
                    sems.at[i],
                )
            )
            copies[-1].start()
        get_scales.wait()
        for i in range(count // chunk):
            copies[i].wait()
            for b in range(units // TILE):
                at = (slice(i * chunk, (i + 1) * chunk), slice(b * TILE, (b + 1) * TILE))
                scale = jnp.full((TILE, TILE), local_ref[blocks[i], b], F32).astype(BF16)
                out_ref[at] = out_ref[at] * scale

    return pl.pallas_call(
        body,
        name="weight_rows",
        out_shape=like(count, units),
        in_specs=[HBM, HBM],
        out_specs=VMEM,
        scratch_shapes=[
            pltpu.SMEM(scales.shape, F32),
            pltpu.SemaphoreType.DMA,
            pltpu.SemaphoreType.DMA((count // chunk,)),
        ],
        compiler_params=pltpu.CompilerParams(vmem_limit_bytes=44 * MIB),
        cost_estimate=pl.CostEstimate(flops=count * units, bytes_accessed=4 * count * units, transcendentals=0),
    )(scales, down_weight)


def grouped(refs, sizes):
    result, at = [], 0
    for size in sizes:
        result.append(refs[at : at + size])
        at += size
    return result


def half_of(piece, h):
    return (piece[0], h * piece[0].shape[0] // 2) if len(piece) == 1 else (piece[h], 0)


def partial_hidden(rows, pieces, weights):
    sizes = [len(p) for p in pieces]
    flat = [a for p in pieces for a in p]
    part = flat[0].shape[1]
    units = weights[0].shape[1]
    each = len(pieces) * rows
    step = 512 if units % 512 == 0 else 256

    def body(*refs):
        weight_refs = refs[len(flat) : len(flat) + len(weights)]
        keep_ref, send_ref, quant_ref = refs[len(flat) + len(weights) :]
        for k, piece in enumerate(grouped(refs, sizes)):
            for h in range(2):
                ref, low = half_of(piece, h)
                for c in range(part // TILE):
                    cols = slice(c * TILE, (c + 1) * TILE)
                    deq = fast_quant(ref[low : low + 2 * rows, cols].astype(F32), 1)
                    into = slice(h * part + c * TILE, h * part + (c + 1) * TILE)
                    for s in range(2):
                        base = s * each + k * rows
                        quant_ref[base : base + rows, into] = deq[s * rows : (s + 1) * rows]
        for i in range(units // step):
            cols = slice(i * step, (i + 1) * step)
            result, at = 0.0, 0
            for ref in weight_refs:
                result += jnp.dot(
                    quant_ref[:, at : at + ref.shape[0]], ref[:, cols], preferred_element_type=F32
                )
                at += ref.shape[0]
            keep_ref[:, cols] = result[:each].astype(keep_ref.dtype)
            send_ref[:, cols] = result[each:].astype(BF16)

    return pl.pallas_call(
        body,
        name="partial_hidden",
        out_shape=[like(each, units, dtype=F32), like(each, units)],
        in_specs=[VMEM] * (len(flat) + len(weights)),
        out_specs=[VMEM] * 2,
        scratch_shapes=[pltpu.VMEM((2 * each, 2 * part), BF16)],
        compiler_params=pltpu.CompilerParams(vmem_limit_bytes=16 * MIB),
        cost_estimate=pl.CostEstimate(
            flops=8 * each * part * units, bytes_accessed=4 * part * units, transcendentals=0
        ),
    )(*flat, *weights)


def hidden_rows(group, rows):
    own, other = group
    for low in range(0, own.shape[0], rows):
        at = (slice(low, low + rows), slice(None))
        yield own[at].astype(F32) + other[at].astype(F32)


def down_product(n_tp, offsets, pieces, others, hiddens, gate_factor, up_factor, groups):
    flat = [p[0] for p in pieces] + list(others)
    part = flat[0].shape[1]
    tokens, units = hiddens[0].shape
    rows = tokens // len(pieces)
    slots, split = 3, 4
    step = 512 if part > 512 else 128
    steps, at = [], 0
    while at < part:
        size = min(step, part - at)
        cut = at + size == part and size > TILE
        steps += [(at, size - TILE), (at + size - TILE, TILE)] if cut else [(at, size)]
        at += size
    widest = max(size for _, size in steps)
    group_arrays = [a for g in groups for a in g]
    early = sum(g[0].shape[0] for g in groups) // rows
    inputs = len(flat) + 4 + 2 + len(group_arrays)
    third = units // 3 if units % (3 * TILE) == 0 else units

    def body(*refs):
        own, other = refs[: len(pieces)], refs[len(pieces) : len(flat)]
        where = [[(ref, s * rows) for ref in own] for s in range(2)]
        where += [
            [(ref, low + s * rows) for ref in other for low in range(0, ref.shape[0], 2 * rows)]
            for s in range(2)
        ]
        h_refs = refs[len(flat) : len(flat) + 4]
        gate_ref, up_ref, *group_refs = refs[len(flat) + 4 : inputs]
        out_ref, gate_out, up_out, token_ref = refs[inputs : inputs + 4]
        hid_ref, quant_ref, buffer, sems, gate_buf, up_buf, row_sems = refs[inputs + 4 :]
        token_ref[...] = jnp.zeros(token_ref.shape, F32)
        starts = [pl.multiple_of(s * rows, rows) for s in ring_sources(n_tp, offsets)]
        for j, ref in enumerate(h_refs):
            for k, start in enumerate(starts):
                low = j * tokens + k * rows
                hid_ref[low : low + rows, :] = ref[pl.ds(start, rows), :]

        def copies(i):
            at, size = steps[i]
            lines = size // split
            return [
                pltpu.make_async_copy(
                    buffer.at[i % slots, pl.ds(k * lines, lines)],
                    out_ref.at[pl.ds(at + k * lines, lines)],
                    sems.at[i % slots, k],
                )
                for k in range(split)
            ]

        row_copies = []
        sums = [r for g in grouped(group_refs, [2] * len(groups)) for r in hidden_rows(g, rows)]
        for k, grad in enumerate(sums):
            there = pl.ds(starts[k], rows)
            here = pl.ds(k * rows, rows)
            gate_buf[here, :] = (grad * gate_ref[there, :]).astype(BF16)
            up_buf[here, :] = (grad * up_ref[there, :]).astype(BF16)
            for h, (buf, out) in enumerate(((gate_buf, gate_out), (up_buf, up_out))):
                row_copies.append(
                    pltpu.make_async_copy(buf.at[here], out.at[there], row_sems.at[h, k])
                )
                row_copies[-1].start()

        for i, (at, size) in enumerate(steps):
            if i >= slots:
                for copy in copies(i - slots):
                    copy.wait()
            for c in range(size // TILE):
                cols = slice(at + c * TILE, at + (c + 1) * TILE)
                for j in range(4):
                    vals = [ref[low : low + rows, cols].astype(F32) for ref, low in where[j]]
                    top = jnp.abs(vals[0])
                    for v in vals[1:]:
                        top = jnp.maximum(top, jnp.abs(v))
                    scale = (jnp.max(top, axis=0, keepdims=True) + 1e-06) / 448.0
                    inverse = 1.0 / scale
                    for k, v in enumerate(vals):
                        payload = (v * inverse).astype(BF16).astype(F32)
                        base = j * tokens + k * rows
                        quant_ref[base : base + rows, c * TILE : (c + 1) * TILE] = (
                            payload * scale
                        ).astype(BF16)
            for low in range(0, units, third):
                hidden = hid_ref[:, low : low + third]
                buffer[i % slots, :size, low : low + third] = lax.dot_general(
                    quant_ref[:, :size], hidden, (((0,), (0,)), ((), ())), preferred_element_type=F32
                ).astype(BF16)
            for copy in copies(i):
                copy.start()
        for i in range(max(0, len(steps) - slots), len(steps)):
            for copy in copies(i):
                copy.wait()
        for copy in row_copies:
            copy.wait()

    return pl.pallas_call(
        body,
        name="down_product",
        out_shape=[like(part, units), like(tokens, units), like(tokens, units), like(8, TILE, dtype=F32)],
        in_specs=[VMEM] * inputs,
        out_specs=[HBM] * 3 + [VMEM],
        scratch_shapes=[
            pltpu.VMEM((4 * tokens, units), BF16),
            pltpu.VMEM((4 * tokens, widest), BF16),
            pltpu.VMEM((slots, widest, units), BF16),
            pltpu.SemaphoreType.DMA((slots, split)),
            pltpu.VMEM((early * rows, units), BF16),
            pltpu.VMEM((early * rows, units), BF16),
            pltpu.SemaphoreType.DMA((2, early)),
        ],
        compiler_params=pltpu.CompilerParams(vmem_limit_bytes=24 * MIB),
        cost_estimate=pl.CostEstimate(
            flops=8 * part * tokens * units, bytes_accessed=2 * part * units, transcendentals=0
        ),
    )(*flat, *hiddens, gate_factor, up_factor, *group_arrays)


def last_step(n_tp, offsets, gate_factor, up_factor, group, gate_grad, up_grad, token):
    tokens, units = gate_factor.shape
    rows = tokens // len(offsets)
    count = group[0].shape[0] // rows

    def body(gate_ref, up_ref, _, own, other, __, ___, gate_out, up_out, gate_buf, up_buf, sems):
        starts = ring_sources(n_tp, offsets[len(offsets) - count :])
        copies = []
        for k, grad in enumerate(hidden_rows((own, other), rows)):
            where = pl.ds(pl.multiple_of(starts[k] * rows, rows), rows)
            here = pl.ds(k * rows, rows)
            gate_buf[here, :] = (grad * gate_ref[where, :]).astype(BF16)
            up_buf[here, :] = (grad * up_ref[where, :]).astype(BF16)
            for h, (buf, out) in enumerate(((gate_buf, gate_out), (up_buf, up_out))):
                copies.append(pltpu.make_async_copy(buf.at[here], out.at[where], sems.at[h, k]))
                copies[-1].start()
        for copy in copies:
            copy.wait()

    return pl.pallas_call(
        body,
        name="last_step",
        out_shape=[like(tokens, units)] * 2,
        in_specs=[VMEM] * 5 + [HBM] * 2,
        out_specs=[HBM] * 2,
        input_output_aliases={5: 0, 6: 1},
        scratch_shapes=[pltpu.VMEM((count * rows, units), BF16)] * 2
        + [pltpu.SemaphoreType.DMA((2, count))],
        compiler_params=pltpu.CompilerParams(vmem_limit_bytes=48 * MIB),
        cost_estimate=pl.CostEstimate(
            flops=8 * tokens * units, bytes_accessed=16 * tokens * units, transcendentals=0
        ),
    )(gate_factor, up_factor, token, *group, gate_grad, up_grad)


def after(value, *others):
    return lax.optimization_barrier((value, *others))[0]


def pair_mesh(n_tp, out_grad, gate_pre, up_pre, down_weight, block_scales):
    half = n_tp // 2
    order = [2 * i for i in range(half)] + [2 * (n_tp - 1 - i) + 1 for i in range(half, n_tp)]
    up = {order[i]: order[(i + 1) % n_tp] for i in range(n_tp)}
    down = {v: k for k, v in up.items()}

    def permute(value, target):
        pairs = []
        for d in range(4):
            for t in range(n_tp):
                dd, tt = target(d, t)
                pairs.append((d * n_tp + t, dd * n_tp + tt))
        return lax.ppermute(value, BOTH, pairs)

    def flip(value, bits):
        return permute(value, lambda d, t: (d ^ bits, t))

    def send_up(value):
        return permute(value, lambda d, t: (d, up[t]))

    def send_down(value):
        return permute(value, lambda d, t: (d, down[t]))

    rows = out_grad.shape[0]
    offsets = [0]
    for k in range(1, half):
        offsets += [k, -k]
    offsets.append(half)

    own, other, send, gate_here, up_here = split_columns(out_grad, gate_pre, up_pre, 4)
    arrived = flip(send, 2)
    scales = after(block_scales, own).astype(F32)
    hidden_own, gate_factor, up_factor = hidden_quant(after(gate_here, scales), up_here)
    part = own.shape[1]
    tiles = 2 * part // 256
    cuts = [0, 256 * (tiles * 3 // 14), 256 * (tiles * 10 // 14), 2 * part]

    def weight_cut(i, *others):
        return weight_rows(down_weight, after(scales, *others), 4, cuts[i], cuts[i + 1] - cuts[i])

    weight0 = weight_cut(0, hidden_own)
    arrived = after(arrived, weight0)
    block = jnp.concatenate([own, arrived[:rows], other, arrived[rows:]], axis=0)
    weight1 = weight_cut(1, block)
    hidden_chip = flip(hidden_own, 2)
    hidden_core = flip(hidden_own, 1)

    got = {0: block}
    for k in range(1, half):
        low, high = got[1 - k], got[k - 1]
        if k == 2:
            low, high = after(low, weight1), after(high, weight1)
            weight2 = weight_cut(2, hidden_core)
            weights = weight0, weight1, weight2
            part1 = partial_hidden(rows, [[got[o]] for o in offsets[:3]], weights)
        if k == 3:
            low, high = after(low, part1[0]), after(high, part1[0])
        got[-k], got[k] = send_up(low), send_down(high)
    first = n_tp - 3
    part2 = partial_hidden(rows, [[got[o]] for o in offsets[3:first]], weights)
    hidden_far = flip(after(hidden_chip, got[1 - half], got[half - 1]), 1)
    last = [send_up(after(got[1 - half], part2[0]))]
    pieces = [[got[o]] for o in offsets[:-1]] + [last]

    sum1 = flip(part1[1], 2)
    sum2 = flip(part2[1], 2)
    other1 = flip(jnp.concatenate([got[o][2 * rows :] for o in offsets[:first]], axis=0), 1)
    late = [after(a, sum1, sum2) for a in last]
    tail = after(late[0], hidden_far)
    other2 = flip(
        jnp.concatenate([got[o][2 * rows :] for o in offsets[first:-1]] + [tail[2 * rows :]], axis=0), 1
    )
    part3 = partial_hidden(rows, pieces[first:-1] + [late], weights)
    sum3 = flip(part3[1], 2)
    down_grad, gate_grad, up_grad, token = down_product(
        n_tp,
        offsets,
        pieces,
        [other1, other2],
        [hidden_own, hidden_chip, hidden_core, hidden_far],
        gate_factor,
        up_factor,
        [(part1[0], sum1), (part2[0], sum2)],
    )
    gate_grad, up_grad = last_step(
        n_tp, offsets, gate_factor, up_factor, (part3[0], sum3), gate_grad, up_grad, token
    )
    return gate_grad, up_grad, down_grad


def solution(mesh):
    n_dp, n_tp = mesh.shape["dp"], mesh.shape["tp"]

    def per_device(out_grad, gate_pre, up_pre, down_weight, block_scales):
        part = down_weight.shape[0] // n_dp
        rows = out_grad.shape[0]
        fits = (
            n_dp == 4
            and n_tp >= 8
            and n_tp % 2 == 0
            and rows % 16 == 0
            and rows * n_tp == 128
            and part % 256 == 0
            and part >= 1024
            and gate_pre.shape[1] % 256 == 0
        )
        if fits:
            return pair_mesh(n_tp, out_grad, gate_pre, up_pre, down_weight, block_scales)
        return any_mesh(out_grad, gate_pre, up_pre, down_weight, block_scales)

    placed = (P(("dp", "tp"), None), P("dp", "tp"), P("dp", "tp"), P(None, "tp"), P(None, "tp"))
    return jax.shard_map(
        per_device,
        mesh=mesh,
        in_specs=placed,
        out_specs=(P("dp", "tp"), P("dp", "tp"), P("dp", "tp")),
        check_vma=False,
    )
```

```python
import jax
import jax.numpy as jnp
from jax import lax
from jax.experimental import pallas as pl
from jax.experimental.pallas import tpu as pltpu
from jax.sharding import PartitionSpec as P

BF16 = jnp.bfloat16
F32 = jnp.float32
BOTH = ("dp", "tp")
TILE = 128


def tile_quant(values, tile_axis):
    largest = jnp.max(jnp.abs(values), axis=tile_axis, keepdims=True)
    tile_scale = (largest + 1e-06) / 448.0
    payload = (values / tile_scale).astype(jnp.bfloat16)
    return (payload.astype(jnp.float32) * tile_scale).astype(jnp.bfloat16)


def fast_quant(values, tile_axis):
    largest = jnp.max(jnp.abs(values), axis=tile_axis, keepdims=True)
    tile_scale = (largest + 1e-06) / 448.0
    payload = (values * (1.0 / tile_scale)).astype(BF16)
    return (payload.astype(F32) * tile_scale).astype(BF16)


def any_mesh(out_grad, gate_pre, up_pre, down_weight, block_scales):
    width = down_weight.shape[0]
    hidden_units = down_weight.shape[1]
    weight_deq = (
        down_weight.reshape(width // 128, 128, hidden_units // 128, 128)
        * block_scales[:, None, :, None]
    ).reshape(width, hidden_units)
    grad_tokens = lax.all_gather(out_grad, "tp", axis=0, tiled=True)
    local_tokens = grad_tokens.shape[0]
    grad_full = grad_tokens.astype(jnp.float32)
    grad_rowq = tile_quant(grad_full.reshape(local_tokens, width // 128, 128), 2).reshape(
        local_tokens, width
    )
    grad_colq = tile_quant(grad_full.reshape(local_tokens // 128, 128, width), 1).reshape(
        local_tokens, width
    )
    hidden_grad = jnp.dot(grad_rowq, weight_deq, preferred_element_type=jnp.float32)
    gate_val = gate_pre.astype(jnp.float32)
    up_val = up_pre.astype(jnp.float32)
    sigma = 1.0 / (1.0 + jnp.exp(-gate_val))
    gate_grad = (hidden_grad * up_val * sigma * (1.0 + gate_val * (1.0 - sigma))).astype(
        jnp.bfloat16
    )
    up_grad = (hidden_grad * gate_val * sigma).astype(jnp.bfloat16)
    hidden_val = gate_val * sigma * up_val
    hidden_colq = tile_quant(hidden_val.reshape(local_tokens // 128, 128, hidden_units), 1).reshape(
        local_tokens, hidden_units
    )
    width_dev = width // lax.axis_size("dp")
    every_cols = lax.all_to_all(grad_colq, "dp", split_axis=1, concat_axis=0, tiled=True)
    start_sum = jnp.zeros((width_dev, hidden_units), jnp.float32)
    hidden_piece = lax.all_gather(hidden_colq, "dp", axis=0, tiled=True)
    block_count = hidden_piece.shape[0] // local_tokens

    def one_block(block_num, inner):
        hidden_block = lax.dynamic_slice_in_dim(
            hidden_piece, block_num * local_tokens, local_tokens, 0
        )
        grad_block = lax.dynamic_slice_in_dim(every_cols, block_num * local_tokens, local_tokens, 0)
        term = lax.dot_general(
            grad_block, hidden_block, (((0,), (0,)), ((), ())), preferred_element_type=jnp.float32
        )
        term = lax.optimization_barrier(term.astype(jnp.bfloat16)).astype(jnp.float32)
        return inner + term

    summed = lax.fori_loop(0, block_count, one_block, start_sum)
    return (gate_grad, up_grad, summed.astype(jnp.bfloat16))


VMEM = pl.BlockSpec(memory_space=pltpu.VMEM)
SMEM = pl.BlockSpec(memory_space=pltpu.SMEM)
HBM = pl.BlockSpec(memory_space=pltpu.HBM)
MIB = 1024 * 1024


def like(*shape, dtype=BF16):
    return jax.ShapeDtypeStruct(shape, dtype)


def ring_sources(n_tp, offsets):
    half = n_tp // 2
    me = lax.axis_index("tp")
    odd = lax.rem(me, 2)
    place = jnp.where(odd == 1, n_tp - 1 - me // 2, me // 2)
    result = []
    for offset in offsets:
        at = lax.rem(place + offset + n_tp, n_tp)
        result.append(jnp.where(at < half, 2 * at, 2 * (n_tp - 1 - at) + 1))
    return result


def split_columns(out_grad, gate_pre, up_pre, parts):
    rows, width = out_grad.shape
    part = width // parts

    def body(grad_ref, gate_ref, up_ref, own, other, send, gate_out, up_out, sems):
        me = lax.axis_index("dp")
        pairs = [
            (grad_ref.at[:, pl.ds(pl.multiple_of((me ^ flips) * part, TILE), part)], target)
            for flips, target in (
                (2, send.at[pl.ds(0, rows)]),
                (3, send.at[pl.ds(rows, rows)]),
                (0, own),
                (1, other),
            )
        ]
        pairs += [(gate_ref, gate_out), (up_ref, up_out)]
        copies = [
            pltpu.make_async_copy(source, target, sems.at[i])
            for i, (source, target) in enumerate(pairs)
        ]
        for copy in copies:
            copy.start()
        for copy in copies:
            copy.wait()

    return pl.pallas_call(
        body,
        name="split_columns",
        out_shape=[pltpu.VMEM((rows, part), BF16)] * 2
        + [pltpu.VMEM((2 * rows, part), BF16)]
        + [pltpu.VMEM(gate_pre.shape, BF16)] * 2,
        in_specs=[HBM] * 3,
        out_specs=[VMEM] * 5,
        scratch_shapes=[pltpu.SemaphoreType.DMA((6,))],
    )(out_grad, gate_pre, up_pre)


def hidden_quant(gate_pre, up_pre):
    tokens, units = gate_pre.shape

    def body(gate_ref, up_ref, hidden_ref, gate_factor, up_factor):
        for c in range(units // TILE):
            at = (slice(None), slice(c * TILE, (c + 1) * TILE))
            gate = gate_ref[at].astype(F32)
            up = up_ref[at].astype(F32)
            sigma = 1.0 / (1.0 + jnp.exp(-gate))
            hidden_ref[at] = fast_quant(gate * sigma * up, 0)
            gate_factor[at] = up * sigma * (1.0 + gate * (1.0 - sigma))
            up_factor[at] = gate * sigma

    return pl.pallas_call(
        body,
        name="hidden_quant",
        out_shape=[like(tokens, units)] + [like(tokens, units, dtype=F32)] * 2,
        in_specs=[VMEM] * 2,
        out_specs=[VMEM] * 3,
        compiler_params=pltpu.CompilerParams(vmem_limit_bytes=16 * MIB),
        cost_estimate=pl.CostEstimate(
            flops=20 * tokens * units, bytes_accessed=14 * tokens * units, transcendentals=tokens * units
        ),
    )(gate_pre, up_pre)


def weight_rows(down_weight, scales, parts, first, count):
    width, units = down_weight.shape
    part = width // parts
    chunk = TILE

    def body(scale_ref, weight_ref, out_ref, local_ref, scale_sem, sems):
        me = lax.axis_index("dp")
        get_scales = pltpu.make_async_copy(scale_ref, local_ref, scale_sem)
        get_scales.start()
        copies, blocks = [], []
        for i in range(count // chunk):
            row = first + i * chunk
            start = pl.multiple_of((me ^ (row // part)) * part + row % part, TILE)
            blocks.append((me ^ (row // part)) * (part // TILE) + row % part // TILE)
            copies.append(
                pltpu.make_async_copy(
                    weight_ref.at[pl.ds(start, chunk)],
                    out_ref.at[pl.ds(i * chunk, chunk)],
                    sems.at[i],
                )
            )
            copies[-1].start()
        get_scales.wait()
        for i in range(count // chunk):
            copies[i].wait()
            for b in range(units // TILE):
                at = (slice(i * chunk, (i + 1) * chunk), slice(b * TILE, (b + 1) * TILE))
                scale = jnp.full((TILE, TILE), local_ref[blocks[i], b], F32).astype(BF16)
                out_ref[at] = out_ref[at] * scale

    return pl.pallas_call(
        body,
        name="weight_rows",
        out_shape=like(count, units),
        in_specs=[HBM, HBM],
        out_specs=VMEM,
        scratch_shapes=[
            pltpu.SMEM(scales.shape, F32),
            pltpu.SemaphoreType.DMA,
            pltpu.SemaphoreType.DMA((count // chunk,)),
        ],
        compiler_params=pltpu.CompilerParams(vmem_limit_bytes=44 * MIB),
        cost_estimate=pl.CostEstimate(flops=count * units, bytes_accessed=4 * count * units, transcendentals=0),
    )(scales, down_weight)


def grouped(refs, sizes):
    result, at = [], 0
    for size in sizes:
        result.append(refs[at : at + size])
        at += size
    return result


def half_of(piece, h):
    return (piece[0], h * piece[0].shape[0] // 2) if len(piece) == 1 else (piece[h], 0)


def partial_hidden(rows, pieces, weights):
    sizes = [len(p) for p in pieces]
    flat = [a for p in pieces for a in p]
    part = flat[0].shape[1]
    units = weights[0].shape[1]
    each = len(pieces) * rows
    step = 256

    def body(*refs):
        weight_refs = refs[len(flat) : len(flat) + len(weights)]
        keep_ref, send_ref, quant_ref = refs[len(flat) + len(weights) :]
        for k, piece in enumerate(grouped(refs, sizes)):
            for h in range(2):
                ref, low = half_of(piece, h)
                for c in range(part // TILE):
                    cols = slice(c * TILE, (c + 1) * TILE)
                    deq = fast_quant(ref[low : low + 2 * rows, cols].astype(F32), 1)
                    into = slice(h * part + c * TILE, h * part + (c + 1) * TILE)
                    for s in range(2):
                        base = s * each + k * rows
                        quant_ref[base : base + rows, into] = deq[s * rows : (s + 1) * rows]
        for i in range(units // step):
            cols = slice(i * step, (i + 1) * step)
            result, at = 0.0, 0
            for ref in weight_refs:
                result += jnp.dot(
                    quant_ref[:, at : at + ref.shape[0]], ref[:, cols], preferred_element_type=F32
                )
                at += ref.shape[0]
            keep_ref[:, cols] = result[:each].astype(keep_ref.dtype)
            send_ref[:, cols] = result[each:].astype(BF16)

    return pl.pallas_call(
        body,
        name="partial_hidden",
        out_shape=[like(each, units, dtype=F32), like(each, units)],
        in_specs=[VMEM] * (len(flat) + len(weights)),
        out_specs=[VMEM] * 2,
        scratch_shapes=[pltpu.VMEM((2 * each, 2 * part), BF16)],
        compiler_params=pltpu.CompilerParams(vmem_limit_bytes=16 * MIB),
        cost_estimate=pl.CostEstimate(
            flops=8 * each * part * units, bytes_accessed=4 * part * units, transcendentals=0
        ),
    )(*flat, *weights)


def hidden_rows(group, rows):
    own, other = group
    for low in range(0, own.shape[0], rows):
        at = (slice(low, low + rows), slice(None))
        yield own[at].astype(F32) + other[at].astype(F32)


def down_product(n_tp, offsets, pieces, others, hiddens, gate_factor, up_factor, groups):
    flat = [p[0] for p in pieces] + list(others)
    part = flat[0].shape[1]
    tokens, units = hiddens[0].shape
    rows = tokens // len(pieces)
    slots, split = 3, 4
    step = 512 if part > 512 else 128
    steps, at = [], 0
    while at < part:
        size = min(step, part - at)
        cut = at + size == part and size > TILE
        steps += [(at, size - TILE), (at + size - TILE, TILE)] if cut else [(at, size)]
        at += size
    widest = max(size for _, size in steps)
    group_arrays = [a for g in groups for a in g]
    early = sum(g[0].shape[0] for g in groups) // rows
    inputs = len(flat) + 4 + 2 + len(group_arrays)
    third = units // 3 if units % (3 * TILE) == 0 else units

    def body(*refs):
        own, other = refs[: len(pieces)], refs[len(pieces) : len(flat)]
        where = [[(ref, s * rows) for ref in own] for s in range(2)]
        where += [
            [(ref, low + s * rows) for ref in other for low in range(0, ref.shape[0], 2 * rows)]
            for s in range(2)
        ]
        h_refs = refs[len(flat) : len(flat) + 4]
        gate_ref, up_ref, *group_refs = refs[len(flat) + 4 : inputs]
        out_ref, gate_out, up_out, token_ref = refs[inputs : inputs + 4]
        hid_ref, quant_ref, buffer, sems, gate_buf, up_buf, row_sems = refs[inputs + 4 :]
        token_ref[...] = jnp.zeros(token_ref.shape, F32)
        starts = [pl.multiple_of(s * rows, rows) for s in ring_sources(n_tp, offsets)]
        for j, ref in enumerate(h_refs):
            for k, start in enumerate(starts):
                low = j * tokens + k * rows
                hid_ref[low : low + rows, :] = ref[pl.ds(start, rows), :]

        def copies(i):
            at, size = steps[i]
            lines = size // split
            return [
                pltpu.make_async_copy(
                    buffer.at[i % slots, pl.ds(k * lines, lines)],
                    out_ref.at[pl.ds(at + k * lines, lines)],
                    sems.at[i % slots, k],
                )
                for k in range(split)
            ]

        row_copies = []
        sums = [r for g in grouped(group_refs, [2] * len(groups)) for r in hidden_rows(g, rows)]
        for k, grad in enumerate(sums):
            there = pl.ds(starts[k], rows)
            here = pl.ds(k * rows, rows)
            gate_buf[here, :] = (grad * gate_ref[there, :]).astype(BF16)
            up_buf[here, :] = (grad * up_ref[there, :]).astype(BF16)
            for h, (buf, out) in enumerate(((gate_buf, gate_out), (up_buf, up_out))):
                row_copies.append(
                    pltpu.make_async_copy(buf.at[here], out.at[there], row_sems.at[h, k])
                )
                row_copies[-1].start()

        for i, (at, size) in enumerate(steps):
            if i >= slots:
                for copy in copies(i - slots):
                    copy.wait()
            for c in range(size // TILE):
                cols = slice(at + c * TILE, at + (c + 1) * TILE)
                for j in range(4):
                    vals = [ref[low : low + rows, cols].astype(F32) for ref, low in where[j]]
                    top = jnp.abs(vals[0])
                    for v in vals[1:]:
                        top = jnp.maximum(top, jnp.abs(v))
                    scale = (jnp.max(top, axis=0, keepdims=True) + 1e-06) / 448.0
                    inverse = 1.0 / scale
                    for k, v in enumerate(vals):
                        payload = (v * inverse).astype(BF16).astype(F32)
                        base = j * tokens + k * rows
                        quant_ref[base : base + rows, c * TILE : (c + 1) * TILE] = (
                            payload * scale
                        ).astype(BF16)
            for low in range(0, units, third):
                hidden = hid_ref[:, low : low + third]
                buffer[i % slots, :size, low : low + third] = lax.dot_general(
                    quant_ref[:, :size], hidden, (((0,), (0,)), ((), ())), preferred_element_type=F32
                ).astype(BF16)
            for copy in copies(i):
                copy.start()
        for i in range(max(0, len(steps) - slots), len(steps)):
            for copy in copies(i):
                copy.wait()
        for copy in row_copies:
            copy.wait()

    return pl.pallas_call(
        body,
        name="down_product",
        out_shape=[like(part, units), like(tokens, units), like(tokens, units), like(8, TILE, dtype=F32)],
        in_specs=[VMEM] * inputs,
        out_specs=[HBM] * 3 + [VMEM],
        scratch_shapes=[
            pltpu.VMEM((4 * tokens, units), BF16),
            pltpu.VMEM((4 * tokens, widest), BF16),
            pltpu.VMEM((slots, widest, units), BF16),
            pltpu.SemaphoreType.DMA((slots, split)),
            pltpu.VMEM((early * rows, units), BF16),
            pltpu.VMEM((early * rows, units), BF16),
            pltpu.SemaphoreType.DMA((2, early)),
        ],
        compiler_params=pltpu.CompilerParams(vmem_limit_bytes=24 * MIB),
        cost_estimate=pl.CostEstimate(
            flops=8 * part * tokens * units, bytes_accessed=2 * part * units, transcendentals=0
        ),
    )(*flat, *hiddens, gate_factor, up_factor, *group_arrays)


def last_step(n_tp, offsets, gate_factor, up_factor, group, gate_grad, up_grad, token):
    tokens, units = gate_factor.shape
    rows = tokens // len(offsets)
    count = group[0].shape[0] // rows

    def body(gate_ref, up_ref, _, own, other, __, ___, gate_out, up_out, gate_buf, up_buf, sems):
        starts = ring_sources(n_tp, offsets[len(offsets) - count :])
        copies = []
        for k, grad in enumerate(hidden_rows((own, other), rows)):
            where = pl.ds(pl.multiple_of(starts[k] * rows, rows), rows)
            here = pl.ds(k * rows, rows)
            gate_buf[here, :] = (grad * gate_ref[where, :]).astype(BF16)
            up_buf[here, :] = (grad * up_ref[where, :]).astype(BF16)
            for h, (buf, out) in enumerate(((gate_buf, gate_out), (up_buf, up_out))):
                copies.append(pltpu.make_async_copy(buf.at[here], out.at[where], sems.at[h, k]))
                copies[-1].start()
        for copy in copies:
            copy.wait()

    return pl.pallas_call(
        body,
        name="last_step",
        out_shape=[like(tokens, units)] * 2,
        in_specs=[VMEM] * 5 + [HBM] * 2,
        out_specs=[HBM] * 2,
        input_output_aliases={5: 0, 6: 1},
        scratch_shapes=[pltpu.VMEM((count * rows, units), BF16)] * 2
        + [pltpu.SemaphoreType.DMA((2, count))],
        compiler_params=pltpu.CompilerParams(vmem_limit_bytes=48 * MIB),
        cost_estimate=pl.CostEstimate(
            flops=8 * tokens * units, bytes_accessed=16 * tokens * units, transcendentals=0
        ),
    )(gate_factor, up_factor, token, *group, gate_grad, up_grad)


def after(value, *others):
    return lax.optimization_barrier((value, *others))[0]


def pair_mesh(n_tp, out_grad, gate_pre, up_pre, down_weight, block_scales):
    half = n_tp // 2
    order = [2 * i for i in range(half)] + [2 * (n_tp - 1 - i) + 1 for i in range(half, n_tp)]
    up = {order[i]: order[(i + 1) % n_tp] for i in range(n_tp)}
    down = {v: k for k, v in up.items()}

    def permute(value, target):
        pairs = []
        for d in range(4):
            for t in range(n_tp):
                dd, tt = target(d, t)
                pairs.append((d * n_tp + t, dd * n_tp + tt))
        return lax.ppermute(value, BOTH, pairs)

    def flip(value, bits):
        return permute(value, lambda d, t: (d ^ bits, t))

    def send_up(value):
        return permute(value, lambda d, t: (d, up[t]))

    def send_down(value):
        return permute(value, lambda d, t: (d, down[t]))

    rows = out_grad.shape[0]
    offsets = [0]
    for k in range(1, half):
        offsets += [k, -k]
    offsets.append(half)

    own, other, send, gate_here, up_here = split_columns(out_grad, gate_pre, up_pre, 4)
    arrived = flip(send, 2)
    scales = after(block_scales, own).astype(F32)
    hidden_own, gate_factor, up_factor = hidden_quant(after(gate_here, scales), up_here)
    part = own.shape[1]
    tiles = 2 * part // 256
    cuts = [0, 256 * (tiles * 3 // 14), 256 * (tiles * 10 // 14), 2 * part]

    def weight_cut(i, *others):
        return weight_rows(down_weight, after(scales, *others), 4, cuts[i], cuts[i + 1] - cuts[i])

    weight0 = weight_cut(0, hidden_own)
    arrived = after(arrived, weight0)
    block = jnp.concatenate([own, arrived[:rows], other, arrived[rows:]], axis=0)
    weight1 = weight_cut(1, block)
    hidden_chip = flip(hidden_own, 2)
    hidden_core = flip(hidden_own, 1)

    got = {0: block}
    for k in range(1, half):
        low, high = got[1 - k], got[k - 1]
        if k == 2:
            low, high = after(low, weight1), after(high, weight1)
            weight2 = weight_cut(2, hidden_core)
            weights = weight0, weight1, weight2
            part1 = partial_hidden(rows, [[got[o]] for o in offsets[:3]], weights)
        if k == 3:
            low, high = after(low, part1[0]), after(high, part1[0])
        got[-k], got[k] = send_up(low), send_down(high)
    first = n_tp - 3
    part2 = partial_hidden(rows, [[got[o]] for o in offsets[3:first]], weights)
    hidden_far = flip(after(hidden_chip, got[1 - half], got[half - 1]), 1)
    last = [send_up(after(got[1 - half], part2[0]))]
    pieces = [[got[o]] for o in offsets[:-1]] + [last]

    sum1 = flip(part1[1], 2)
    sum2 = flip(part2[1], 2)
    other1 = flip(jnp.concatenate([got[o][2 * rows :] for o in offsets[:first]], axis=0), 1)
    late = [after(a, sum1, sum2) for a in last]
    tail = after(late[0], hidden_far)
    other2 = flip(
        jnp.concatenate([got[o][2 * rows :] for o in offsets[first:-1]] + [tail[2 * rows :]], axis=0), 1
    )
    part3 = partial_hidden(rows, pieces[first:-1] + [late], weights)
    sum3 = flip(part3[1], 2)
    down_grad, gate_grad, up_grad, token = down_product(
        n_tp,
        offsets,
        pieces,
        [other1, other2],
        [hidden_own, hidden_chip, hidden_core, hidden_far],
        gate_factor,
        up_factor,
        [(part1[0], sum1), (part2[0], sum2)],
    )
    gate_grad, up_grad = last_step(
        n_tp, offsets, gate_factor, up_factor, (part3[0], sum3), gate_grad, up_grad, token
    )
    return gate_grad, up_grad, down_grad


def solution(mesh):
    n_dp, n_tp = mesh.shape["dp"], mesh.shape["tp"]

    def per_device(out_grad, gate_pre, up_pre, down_weight, block_scales):
        part = down_weight.shape[0] // n_dp
        rows = out_grad.shape[0]
        fits = (
            n_dp == 4
            and n_tp >= 8
            and n_tp % 2 == 0
            and rows % 16 == 0
            and rows * n_tp == 128
            and part % 256 == 0
            and part >= 1024
            and gate_pre.shape[1] % 256 == 0
        )
        if fits:
            return pair_mesh(n_tp, out_grad, gate_pre, up_pre, down_weight, block_scales)
        return any_mesh(out_grad, gate_pre, up_pre, down_weight, block_scales)

    placed = (P(("dp", "tp"), None), P("dp", "tp"), P("dp", "tp"), P(None, "tp"), P(None, "tp"))
    return jax.shard_map(
        per_device,
        mesh=mesh,
        in_specs=placed,
        out_specs=(P("dp", "tp"), P("dp", "tp"), P("dp", "tp")),
        check_vma=False,
    )
```
